32 devices in a mesh: dp: 8 (over z, core), expert: 4 (over y, x).
Axes of the slice: x: 2, y: 2, z: 4, core: 2. Of those that a mesh axis runs over, the one named last changes fastest.
Arguments:
- features: bfloat16 [1024, 1024], P('dp'), may hold values from -6 to 6
- cross_weight: bfloat16 [1, 1024, 1024], replicated, may hold values from -0.1875 to 0.1875
- cross_bias: float32 [1, 1024], replicated, may hold values from -3 to 3
- gate_weight: bfloat16 [1024, 64], replicated, may hold values from -0.1875 to 0.1875
- gate_offset: float32 [64], replicated, may hold values from -3 to 3
- up_weight: bfloat16 [16, 1024, 8192], P('expert', None, 'dp'), may hold values from -0.1875 to 0.1875
- down_weight: bfloat16 [16, 8192, 1024], P('expert', 'dp'), may hold values from -0.0625 to 0.0625
- task_grad: bfloat16 [1024, 4, 1024], P('dp'), may hold values from -6 to 6
Outputs:
- task_mixed: bfloat16 [1024, 4, 1024], P('dp')
- feature_grad: bfloat16 [1024, 1024], P('dp')
- up_grad: bfloat16 [16, 1024, 8192], P('expert', None, 'dp')
- down_grad: bfloat16 [16, 8192, 1024], P('expert', 'dp')
- cross_grad: float32 [1, 1024, 1024], replicated
- bias_grad: float32 [1, 1024], replicated
- gating_grad: float32 [1024, 64], replicated
- offset_grad: float32 [64], replicated
The draws below stay inside these ranges and needn't reach their ends.
All inputs are finite; a program needn't handle non-finite values.
Results may differ from the reference program's by a relative error of at most 0.012.
Values may be sent and summed in bfloat16 or wider, within the bound.
No kernel may reach another device: no remote copies, remote signals or barrier semaphores. Data moves between devices by JAX's collectives and lax.ppermute only.
A program may use at most 192 MiB of HBM per device.

```python
import jax
import jax.numpy as jnp
from jax import lax

D = 1024
HIDDEN_SIZE = 8192
EXPERTS = 16
TASKS = 4
LAYERS = 1
ROWS = 1024


def block_scale(stream_key, dims, shards, least, high):
    def one(dim, blocks):
        steps = jax.random.uniform(jax.random.fold_in(jax.random.fold_in(stream_key, 6), dim), (blocks,), jnp.float32, least / len(shards), high / len(shards))
        return jnp.repeat(jnp.exp(steps), dims[dim] // blocks).reshape((-1,) + (1,) * (len(dims) - dim - 1))

    level = one(*shards[0])
    for cut in shards[1:]:
        level = level * one(*cut)
    return level


def normal_values(stream_key, shape, spread, bound, split=(), kind=jnp.bfloat16):
    array = spread * jax.random.normal(stream_key, shape, jnp.float32)
    if split:
        array = array * block_scale(stream_key, shape, split, -0.22, 0.18)
    return jnp.clip(array, -bound, bound).astype(kind)


def setup_inputs(seed: int = 0) -> dict:
    key_list = jax.random.split(jax.random.key(seed), 9)
    return {
        "features": normal_values(key_list[0], (ROWS, D), 1.0, 6.0, ((0, 8),)),
        "cross_weight": normal_values(key_list[1], (LAYERS, D, D), D ** -0.5, 0.1875),
        "cross_bias": normal_values(key_list[2], (LAYERS, D), 0.5, 3.0, (), jnp.float32),
        "gate_weight": normal_values(key_list[3], (D, TASKS * EXPERTS), D ** -0.5, 0.1875),
        "gate_offset": normal_values(key_list[4], (TASKS * EXPERTS,), 1.0, 3.0, (), jnp.float32),
        "up_weight": normal_values(key_list[5], (EXPERTS, D, HIDDEN_SIZE), D ** -0.5, 0.1875, ((0, 4), (2, 8))),
        "down_weight": normal_values(key_list[6], (EXPERTS, HIDDEN_SIZE, D), HIDDEN_SIZE ** -0.5, 0.0625, ((0, 4), (1, 8))),
        "task_grad": normal_values(key_list[7], (ROWS, TASKS, D), 1.0, 6.0, ((0, 8),)),
    }


def cross_forward(features, cross_weight, cross_bias):
    states = features.astype(jnp.float32)
    rounded = []
    updates = []
    for layer in range(cross_weight.shape[0]):
        low = states.astype(jnp.bfloat16)
        update = jnp.dot(low, cross_weight[layer], preferred_element_type=jnp.float32) + cross_bias[layer]
        states = features.astype(jnp.float32) * update + states
        rounded.append(low)
        updates.append(update)
    return states, rounded, updates


def cross_backward(features, cross_weight, rounded, updates, upstream):
    base = features.astype(jnp.float32)
    direct = jnp.zeros_like(upstream)
    weight_terms = []
    bias_terms = []
    for layer in reversed(range(len(rounded))):
        scaled = (upstream * base).astype(jnp.bfloat16)
        weight_terms.insert(0, jnp.dot(rounded[layer].T, scaled, preferred_element_type=jnp.float32))
        bias_terms.insert(0, jnp.sum(scaled.astype(jnp.float32), axis=0))
        direct = direct + upstream * updates[layer]
        upstream = upstream + jnp.dot(scaled, cross_weight[layer].T, preferred_element_type=jnp.float32)
    return (upstream + direct).astype(jnp.bfloat16), jnp.stack(weight_terms), jnp.stack(bias_terms)


def gating(shared, gate_weight, gate_offset):
    logits = jnp.dot(shared, gate_weight, preferred_element_type=jnp.float32) + gate_offset
    logits = logits.reshape(shared.shape[0], TASKS, EXPERTS)
    expo = jnp.exp(logits)
    return expo / jnp.sum(expo, axis=-1, keepdims=True)


def reference(features, cross_weight, cross_bias, gate_weight, gate_offset, up_weight, down_weight, task_grad):
    states, rounded, updates = cross_forward(features, cross_weight, cross_bias)
    shared = states.astype(jnp.bfloat16)
    gate_probs = gating(shared, gate_weight, gate_offset)
    row_count = shared.shape[0]

    def expert_forward(carry, weights):
        hidden_pre = jnp.dot(shared, weights[0], preferred_element_type=jnp.float32)
        hidden_act = (hidden_pre * jax.nn.sigmoid(hidden_pre)).astype(jnp.bfloat16)
        summed = jnp.dot(hidden_act, weights[1], preferred_element_type=jnp.float32)
        return carry, summed

    unused, expert_out = lax.scan(expert_forward, jnp.float32(0.0), (up_weight, down_weight))
    high = lax.Precision.HIGHEST
    task_mixed = jnp.einsum('rte,erd->rtd', gate_probs, expert_out, precision=high).astype(jnp.bfloat16)
    grad_wide = task_grad.astype(jnp.float32)
    out_grad = jnp.einsum('rte,rtd->erd', gate_probs, grad_wide, precision=high).astype(jnp.bfloat16)
    gate_grad = jnp.einsum('rtd,erd->rte', grad_wide, expert_out, precision=high)
    logit_grad = gate_probs * (gate_grad - jnp.sum(gate_probs * gate_grad, axis=-1, keepdims=True))
    logit_low = logit_grad.reshape(row_count, TASKS * EXPERTS).astype(jnp.bfloat16)

    def expert_backward(carry, weights):
        first, second, grad_out = weights
        hidden_pre = jnp.dot(shared, first, preferred_element_type=jnp.float32)
        sig = jax.nn.sigmoid(hidden_pre)
        hidden_act = (hidden_pre * sig).astype(jnp.bfloat16)
        hidden_grad = jnp.dot(grad_out, second.T, preferred_element_type=jnp.float32)
        pre_grad = (hidden_grad * sig * (1.0 + hidden_pre * (1.0 - sig))).astype(jnp.bfloat16)
        second_grad = jnp.dot(hidden_act.T, grad_out, preferred_element_type=jnp.float32).astype(jnp.bfloat16)
        first_grad = jnp.dot(shared.T, pre_grad, preferred_element_type=jnp.float32).astype(jnp.bfloat16)
        carry = carry + jnp.dot(pre_grad, first.T, preferred_element_type=jnp.float32)
        return carry, (first_grad, second_grad)

    start_grad = jnp.zeros(shared.shape, jnp.float32)
    shared_grad, grads = lax.scan(expert_backward, start_grad, (up_weight, down_weight, out_grad))
    shared_grad = shared_grad + jnp.dot(logit_low, gate_weight.T, preferred_element_type=jnp.float32)
    gating_grad = jnp.dot(shared.T, logit_low, preferred_element_type=jnp.float32)
    offset_grad = jnp.sum(logit_grad.reshape(row_count, TASKS * EXPERTS), axis=0)
    feature_grad, cross_grad, bias_grad = cross_backward(features, cross_weight, rounded, updates, shared_grad)
    return (task_mixed, feature_grad, grads[0], grads[1], cross_grad, bias_grad, gating_grad, offset_grad)
```

```python
import functools

import jax
import jax.numpy as jnp
from jax import lax
from jax.experimental import pallas as pl
from jax.experimental.pallas import tpu as pltpu
from jax.sharding import PartitionSpec as P

F32 = jnp.float32
BF16 = jnp.bfloat16
HIGH = lax.Precision.HIGHEST
NN = (((1,), (0,)), ((), ()))
NT = (((1,), (1,)), ((), ()))
TN = (((0,), (0,)), ((), ()))
VMEM_LIMIT = 56 * 2**20


def mm(a, b, dims=NN):
    return lax.dot_general(a, b, dims, preferred_element_type=F32)


def group_sum(values, experts):
    n = values.shape[1]
    same = (
        lax.broadcasted_iota(jnp.int32, (n, n), 0) // experts
        == lax.broadcasted_iota(jnp.int32, (n, n), 1) // experts
    )
    return lax.dot_general(
        values, same.astype(F32), NN, precision=HIGH, preferred_element_type=F32
    )


def column(values, index):
    lane = lax.broadcasted_iota(jnp.int32, values.shape, 1)
    return jnp.sum(jnp.where(lane == index, values, 0.0), axis=1, keepdims=True)


def forward_kernel(
    tasks, experts, sub,
    first_ref, feat_ref, cw_ref, cb_ref, gw_ref, go_ref, up_ref, down_ref,
    shared_ref, gates_ref, act_ref, slope_ref, out_ref, keep_ref, send_ref, acc_ref,
):
    e = pl.program_id(0)
    rows = feat_ref.shape[0]

    @pl.when(e == 0)
    def _():
        for r in range(0, rows, sub):
            part = pl.ds(r, sub)
            base = feat_ref[part, :]
            wide = base.astype(F32)
            update = mm(base, cw_ref[...]) + cb_ref[...]
            shared = (wide * update + wide).astype(BF16)
            shared_ref[part, :] = shared
            expo = jnp.exp(mm(shared, gw_ref[...]) + go_ref[...])
            gates_ref[part, :] = expo / group_sum(expo, experts)
        acc_ref[...] = jnp.zeros_like(acc_ref)

    for r in range(0, rows, sub):
        part = pl.ds(r, sub)
        pre = mm(shared_ref[part, :], up_ref[0])
        sig = jax.nn.sigmoid(pre)
        act = pre * sig
        low = act.astype(BF16)
        act_ref[0, part, :] = low
        slope_ref[0, part, :] = (sig + act * (1.0 - sig)).astype(BF16)
        out = mm(low, down_ref[0])
        out_ref[0, part, :] = out.astype(BF16)
        gates = gates_ref[part, :]
        for t in range(tasks):
            acc_ref[t, part, :] += column(gates, t * experts + first_ref[0] + e) * out

    @pl.when(e == pl.num_programs(0) - 1)
    def _():
        keep_ref[...] = acc_ref[:, : rows // 2, :].astype(BF16)
        send_ref[...] = acc_ref[:, rows // 2 :, :].astype(BF16)


def forward(first, feat, cw, cb, gw, go, up, down, tasks):
    rows, d = feat.shape
    local, _, hid = up.shape
    cols = gw.shape[1]
    experts = cols // tasks
    sub = min(rows, 256)
    whole = lambda e, f: (0, 0)
    by_expert = lambda e, f: (e, 0, 0)
    half = lambda e, f: (0, 0, 0)
    wide = jax.ShapeDtypeStruct((local, rows, hid), BF16)
    grid = pltpu.PrefetchScalarGridSpec(
        num_scalar_prefetch=1,
        grid=(local,),
        in_specs=[
            pl.BlockSpec((rows, d), whole),
            pl.BlockSpec((d, d), whole),
            pl.BlockSpec((1, d), whole),
            pl.BlockSpec((d, cols), whole),
            pl.BlockSpec((1, cols), whole),
            pl.BlockSpec((1, d, hid), by_expert),
            pl.BlockSpec((1, hid, d), by_expert),
        ],
        out_specs=[
            pl.BlockSpec((rows, d), whole),
            pl.BlockSpec((rows, cols), whole),
            pl.BlockSpec((1, rows, hid), by_expert),
            pl.BlockSpec((1, rows, hid), by_expert),
            pl.BlockSpec((1, rows, d), by_expert),
            pl.BlockSpec((tasks, rows // 2, d), half),
            pl.BlockSpec((tasks, rows // 2, d), half),
        ],
        scratch_shapes=[pltpu.VMEM((tasks, rows, d), F32)],
    )
    return pl.pallas_call(
        functools.partial(forward_kernel, tasks, experts, sub),
        grid_spec=grid,
        out_shape=[
            jax.ShapeDtypeStruct((rows, d), BF16),
            jax.ShapeDtypeStruct((rows, cols), F32),
            wide,
            wide,
            jax.ShapeDtypeStruct((local, rows, d), BF16),
            jax.ShapeDtypeStruct((tasks, rows // 2, d), BF16),
            jax.ShapeDtypeStruct((tasks, rows // 2, d), BF16),
        ],
        compiler_params=pltpu.CompilerParams(vmem_limit_bytes=VMEM_LIMIT),
        cost_estimate=pl.CostEstimate(
            flops=4 * rows * d * hid * local, bytes_accessed=2**24, transcendentals=0
        ),
        name="forward",
    )(first, feat, cw, cb, gw, go, up, down)


def backward_kernel(
    tasks, experts, block, places, n_grads,
    first_ref, *refs,
):
    grads = refs[:n_grads]
    gates_ref, out_ref, slope_ref, up_ref, down_ref = refs[n_grads : n_grads + 5]
    og_ref, pg_ref, keep_ref, send_ref, acc_ref, inner_ref = refs[n_grads + 5 :]
    e = pl.program_id(0)
    rows, d = acc_ref.shape
    cols = gates_ref.shape[1]

    @pl.when(e == 0)
    def _():
        acc_ref[...] = jnp.zeros_like(acc_ref)
        inner_ref[...] = jnp.zeros_like(inner_ref)

    for i, (which, lead) in enumerate(places):
        part = pl.ds(i * block, block)
        gates = gates_ref[part, :]
        expert_out = out_ref[0, part, :].astype(F32)
        lane = lax.broadcasted_iota(jnp.int32, gates.shape, 1)
        total = None
        inner = inner_ref[part, :]
        for t in range(tasks):
            col = t * experts + first_ref[0] + e
            grad = grads[which][lead, t].astype(F32)
            term = column(gates, col) * grad
            total = term if total is None else total + term
            dot = jnp.sum(grad * expert_out, axis=1, keepdims=True)
            inner = jnp.where(lane == col, dot, inner)
        inner_ref[part, :] = inner
        og_ref[0, part, :] = total.astype(BF16)

    sub = min(rows, 256)
    for r in range(0, rows, sub):
        part = pl.ds(r, sub)
        hidden = mm(og_ref[0, part, :], down_ref[0], NT)
        pre_grad = (hidden * slope_ref[0, part, :].astype(F32)).astype(BF16)
        pg_ref[0, part, :] = pre_grad
        acc_ref[part, :] += mm(pre_grad, up_ref[0], NT)

    @pl.when(e == pl.num_programs(0) - 1)
    def _():
        half = rows // 2
        gates = gates_ref[...]
        inner = inner_ref[...]
        logit = gates * (inner - group_sum(gates * inner, experts))
        high = logit.astype(BF16)
        low = (logit - high.astype(F32)).astype(BF16)
        row = lax.broadcasted_iota(jnp.int32, (cols, 2 * cols), 0)
        lane = lax.broadcasted_iota(jnp.int32, (cols, 2 * cols), 1)
        pair = mm(high, (lane == row).astype(BF16)) + mm(low, (lane == row + cols).astype(BF16))
        pair = pair.astype(BF16)
        for ref, lo in ((keep_ref, 0), (send_ref, half)):
            ref[:, :d] = acc_ref[lo : lo + half, :].astype(BF16)
            ref[:, d:] = pair[lo : lo + half, :]


def backward(first, grads, places, gates, out, slope, up, down):
    local, rows, d = out.shape
    hid = up.shape[2]
    tasks, block = grads[0].shape[1:3]
    cols = gates.shape[1]
    experts = cols // tasks
    whole = lambda e, f: (0, 0)
    by_expert = lambda e, f: (e, 0, 0)
    grid = pltpu.PrefetchScalarGridSpec(
        num_scalar_prefetch=1,
        grid=(local,),
        in_specs=[pl.BlockSpec(g.shape, lambda e, f: (0, 0, 0, 0)) for g in grads]
        + [
            pl.BlockSpec((rows, cols), whole),
            pl.BlockSpec((1, rows, d), by_expert),
            pl.BlockSpec((1, rows, hid), by_expert),
            pl.BlockSpec((1, d, hid), by_expert),
            pl.BlockSpec((1, hid, d), by_expert),
        ],
        out_specs=[
            pl.BlockSpec((1, rows, d), by_expert),
            pl.BlockSpec((1, rows, hid), by_expert),
            pl.BlockSpec((rows // 2, d + 2 * cols), whole),
            pl.BlockSpec((rows // 2, d + 2 * cols), whole),
        ],
        scratch_shapes=[pltpu.VMEM((rows, d), F32), pltpu.VMEM((rows, cols), F32)],
    )
    return pl.pallas_call(
        functools.partial(backward_kernel, tasks, experts, block, places, len(grads)),
        grid_spec=grid,
        out_shape=[
            jax.ShapeDtypeStruct((local, rows, d), BF16),
            jax.ShapeDtypeStruct((local, rows, hid), BF16),
            jax.ShapeDtypeStruct((rows // 2, d + 2 * cols), BF16),
            jax.ShapeDtypeStruct((rows // 2, d + 2 * cols), BF16),
        ],
        compiler_params=pltpu.CompilerParams(vmem_limit_bytes=VMEM_LIMIT),
        cost_estimate=pl.CostEstimate(
            flops=4 * rows * d * hid * local, bytes_accessed=2**24, transcendentals=0
        ),
        name="backward",
    )(first, *grads, gates, out, slope, up, down)


def weights_kernel(n, *refs):
    shared, acts, ogs, pgs = refs[:n], refs[n : 2 * n], refs[2 * n : 3 * n], refs[3 * n : 4 * n]
    up_ref, down_ref = refs[4 * n :]
    total = mm(shared[0][...], pgs[0][0], TN)
    for i in range(1, n):
        total += mm(shared[i][...], pgs[i][0], TN)
    up_ref[0] = total.astype(BF16)
    total = mm(acts[0][0], ogs[0][0], TN)
    for i in range(1, n):
        total += mm(acts[i][0], ogs[i][0], TN)
    down_ref[0] = total.astype(BF16)


def weight_grads(shared, acts, ogs, pgs):
    local, _, hid = acts[0].shape
    d = shared[0].shape[1]
    rows = sum(s.shape[0] for s in shared)
    by_expert = lambda e: (e, 0, 0)
    return pl.pallas_call(
        functools.partial(weights_kernel, len(shared)),
        grid=(local,),
        in_specs=[pl.BlockSpec(s.shape, lambda e: (0, 0)) for s in shared]
        + [pl.BlockSpec((1,) + x.shape[1:], by_expert) for x in (*acts, *ogs, *pgs)],
        out_specs=[
            pl.BlockSpec((1, d, hid), by_expert),
            pl.BlockSpec((1, hid, d), by_expert),
        ],
        out_shape=[
            jax.ShapeDtypeStruct((local, d, hid), BF16),
            jax.ShapeDtypeStruct((local, hid, d), BF16),
        ],
        compiler_params=pltpu.CompilerParams(vmem_limit_bytes=VMEM_LIMIT),
        cost_estimate=pl.CostEstimate(
            flops=4 * rows * d * hid * local, bytes_accessed=2**25, transcendentals=0
        ),
        name="weight_grads",
    )(*shared, *acts, *ogs, *pgs)


class Ring:
    def __init__(self, dp, expert):
        size = dp * expert

        def pairs(move):
            found = []
            for i in range(size):
                z, c, x = i // expert // 2, i // expert % 2, i % expert
                z, c, x = move(z, c, x)
                found.append((i, (z * 2 + c) * expert + x))
            return found

        near, far = (1, 3), (3, 1)
        self.core_pairs = pairs(lambda z, c, x: (z, 1 - c, x))
        self.a_pairs = pairs(lambda z, c, x: (z ^ near[c], c, x))
        self.b_pairs = pairs(lambda z, c, x: (z ^ far[c], c, x))
        self.e1_pairs = pairs(lambda z, c, x: (z, c, x ^ (1, 2)[c]))
        self.e2_pairs = pairs(lambda z, c, x: (z, c, x ^ (2, 1)[c]))

    def move(self, x, pairs):
        return lax.ppermute(x, ("dp", "expert"), pairs)

    def gather(self, x):
        core = self.core_pairs
        own = jnp.stack([x, self.move(x, core)])
        a = self.move(own, self.a_pairs)
        b = self.move(a, core)
        ab = self.move(b[1], self.a_pairs)
        return own, a, b, ab, self.move(ab, core)

    def places(self):
        return (
            ((0,), ((0, 0), (0, 1))),
            ((1, 2), ((0, 0), (1, 1), (0, 1), (1, 0))),
            ((3, 4), ((0, 0), (1, 0))),
        )

    def chunks(self, parts):
        own, a, b, ab, ba = parts
        return [(own,), (a, b), (ab[None], ba[None])]

    def reduce(self, keep, send, rows_dim):
        got = [self.move(s, self.core_pairs) for s in send]

        def cut(x, i):
            n = x.shape[rows_dim] // 2
            return lax.slice_in_dim(x, i * n, (i + 1) * n, axis=rows_dim).astype(F32)

        own = keep[0].astype(F32) + got[0].astype(F32)
        a = cut(keep[1], 0) + cut(got[1], 1)
        b = cut(keep[1], 1) + cut(got[1], 0)
        ab = keep[2].astype(F32) + got[2].astype(F32)
        got = self.move(jnp.stack([a, ab]).astype(BF16), self.a_pairs).astype(F32)
        own, b = own + got[0], b + got[1]
        own = own + self.move(b.astype(BF16), self.b_pairs).astype(F32)
        own = own + self.move(own.astype(BF16), self.e1_pairs).astype(F32)
        return own + self.move(own.astype(BF16), self.e2_pairs).astype(F32)


class Plain:
    def __init__(self, dp, expert):
        self.dp = dp

    def gather(self, x):
        return lax.all_gather(x, "dp", axis=0)

    def count(self):
        return 4 if self.dp % 4 == 0 else 1

    def places(self):
        n = self.dp // self.count()
        return tuple(((0,), tuple((0, i) for i in range(n))) for _ in range(self.count()))

    def chunks(self, parts):
        n = self.dp // self.count()
        return [(parts[i * n : (i + 1) * n],) for i in range(self.count())]

    def reduce(self, keep, send, rows_dim):
        rows = jnp.concatenate(
            [x for pair in zip(keep, send) for x in pair], axis=rows_dim
        ).astype(F32)
        own = lax.psum_scatter(rows, "dp", scatter_dimension=rows_dim, tiled=True)
        return lax.psum(own, "expert")


def lay(parts, places):
    return jnp.concatenate([parts[which][lead] for which, lead in places], axis=0)


def local_step(
    net, features, cross_weight, cross_bias, gate_weight, gate_offset, up_weight, down_weight,
    task_grad,
):
    d = features.shape[1]
    tasks = task_grad.shape[1]
    cols = gate_weight.shape[1]
    first = (lax.axis_index("expert") * up_weight.shape[0]).astype(jnp.int32).reshape(1)
    places = [p for _, p in net.places()]

    feats = [lay(parts, p) for parts, p in zip(net.chunks(net.gather(features)), places)]
    grads = net.chunks(net.gather(jnp.transpose(task_grad, (1, 0, 2))))

    done = [
        forward(
            first, f, cross_weight[0], cross_bias, gate_weight, gate_offset[None], up_weight,
            down_weight, tasks,
        )
        for f in feats
    ]
    shared, gates, acts, slopes, outs, keeps, sends = zip(*done)
    back = [
        backward(first, g, p, gt, o, s, up_weight, down_weight)
        for g, p, gt, o, s in zip(grads, places, gates, outs, slopes)
    ]
    ogs, pgs, grad_keeps, grad_sends = zip(*back)
    mixed = net.reduce(keeps, sends, 1)
    total = net.reduce(grad_keeps, grad_sends, 0)
    up_grad, down_grad = weight_grads(shared, acts, ogs, pgs)

    task_mixed = jnp.transpose(mixed.astype(BF16), (1, 0, 2))

    wide = features.astype(F32)
    update = mm(features, cross_weight[0]) + cross_bias
    logit = total[:, d : d + cols] + total[:, d + cols :]
    upstream = total[:, :d] + mm(logit.astype(BF16), gate_weight, NT)
    scaled = (upstream * wide).astype(BF16)
    feature_grad = (upstream + mm(scaled, cross_weight[0], NT) + upstream * update).astype(BF16)
    high = logit.astype(BF16)
    low = (logit - high.astype(F32)).astype(BF16)
    tail = net.chunks(net.gather(jnp.concatenate([scaled, high, low], axis=1)))
    tail = jnp.concatenate([lay(parts, p) for parts, p in zip(tail, places)], axis=0)
    scaled = tail[:, :d]
    cross_grad = mm(jnp.concatenate(feats, axis=0), scaled, TN)
    bias_grad = jnp.sum(scaled.astype(F32), axis=0)
    high, low = tail[:, d : d + cols], tail[:, d + cols :]
    gating_grad = mm(jnp.concatenate(shared, axis=0), high, TN)
    offset_grad = jnp.sum(high.astype(F32) + low.astype(F32), axis=0)
    return (
        task_mixed,
        feature_grad,
        up_grad,
        down_grad,
        cross_grad[None],
        bias_grad[None],
        gating_grad,
        offset_grad,
    )


def solution(mesh):
    dp, expert = mesh.shape["dp"], mesh.shape["expert"]
    net = (Ring if (dp, expert) == (8, 4) else Plain)(dp, expert)
    return jax.shard_map(
        functools.partial(local_step, net),
        mesh=mesh,
        in_specs=(
            P("dp", None),
            P(),
            P(),
            P(),
            P(),
            P("expert", None, "dp"),
            P("expert", "dp", None),
            P("dp", None, None),
        ),
        out_specs=(
            P("dp", None, None),
            P("dp", None),
            P("expert", None, "dp"),
            P("expert", "dp", None),
            P(),
            P(),
            P(),
            P(),
        ),
        check_vma=False,
    )
```

```python
import functools

import jax
import jax.numpy as jnp
from jax import lax
from jax.experimental import pallas as pl
from jax.experimental.pallas import tpu as pltpu
from jax.sharding import PartitionSpec as P

F32 = jnp.float32
BF16 = jnp.bfloat16
NN = (((1,), (0,)), ((), ()))
NT = (((1,), (1,)), ((), ()))
TN = (((0,), (0,)), ((), ()))
VMEM_LIMIT = 56 * 2**20
FORWARD_PARTS = 4
WEIGHT_PARTS = 2


def mm(a, b, dims=NN):
    return lax.dot_general(a, b, dims, preferred_element_type=F32)


def exact(values, ones):
    high = values.astype(BF16)
    low = (values - high.astype(F32)).astype(BF16)
    return mm(high, ones) + mm(low, ones)


def shift(values, size):
    assert size & (size - 1) == 0
    return lax.shift_right_logical(values, jnp.int32(size.bit_length() - 1))


def group_sum(values, experts):
    n = values.shape[1]
    row = shift(lax.broadcasted_iota(jnp.int32, (n, n), 0), experts)
    lane = shift(lax.broadcasted_iota(jnp.int32, (n, n), 1), experts)
    return exact(values, jnp.where(row == lane, 1.0, 0.0).astype(BF16))


def params(flops, name):
    return dict(
        compiler_params=pltpu.CompilerParams(vmem_limit_bytes=VMEM_LIMIT),
        cost_estimate=pl.CostEstimate(flops=flops, bytes_accessed=2**22, transcendentals=0),
        name=name,
    )


def cross_kernel(experts, sub, feat_ref, cw_ref, cb_ref, gw_ref, go_ref, shared_ref, gates_ref):
    for r in range(0, feat_ref.shape[0], sub):
        part = pl.ds(r, sub)
        base = feat_ref[part, :]
        wide = base.astype(F32)
        update = mm(base, cw_ref[...]) + cb_ref[...]
        shared = (wide * update + wide).astype(BF16)
        shared_ref[part, :] = shared
        expo = jnp.exp(mm(shared, gw_ref[...]) + go_ref[...])
        gates_ref[part, :] = expo / group_sum(expo, experts)


def cross(feat, cw, cb, gw, go, tasks):
    rows, d = feat.shape
    cols = gw.shape[1]
    sub = 256
    whole = lambda i: (0, 0)
    return pl.pallas_call(
        functools.partial(cross_kernel, cols // tasks, sub),
        grid=(rows // sub,),
        in_specs=[
            pl.BlockSpec((sub, d), lambda i: (i, 0)),
            pl.BlockSpec((d, d), whole),
            pl.BlockSpec((1, d), whole),
            pl.BlockSpec((d, cols), whole),
            pl.BlockSpec((1, cols), whole),
        ],
        out_specs=[
            pl.BlockSpec((sub, d), lambda i: (i, 0)),
            pl.BlockSpec((sub, cols), lambda i: (i, 0)),
        ],
        out_shape=[
            jax.ShapeDtypeStruct((rows, d), BF16),
            jax.ShapeDtypeStruct((rows, cols), F32),
        ],
        **params(2 * rows * d * d, "cross"),
    )(feat, cw, cb, gw, go)


def forward_kernel(shared_ref, up_ref, down_ref, *refs):
    act_ref, slope_ref, out_ref = refs[-3:]
    pre = mm(shared_ref[...], up_ref[0])
    sig = jax.nn.sigmoid(pre)
    act = pre * sig
    low = act.astype(BF16)
    act_ref[0] = low
    slope_ref[0] = (sig + act * (1.0 - sig)).astype(BF16)
    out_ref[0] = mm(low, down_ref[0]).astype(BF16)


def forward(shared, up, down, begin, count, before):
    rows, d = shared.shape
    local, _, hid = up.shape
    sub = min(rows, 512)
    here = lambda e, r: (begin + e, r, 0)
    there = lambda e, r: (begin + e, 0, 0)
    wide = jax.ShapeDtypeStruct((local, rows, hid), BF16)
    return pl.pallas_call(
        forward_kernel,
        grid=(count, rows // sub),
        in_specs=[
            pl.BlockSpec((sub, d), lambda e, r: (r, 0)),
            pl.BlockSpec((1, d, hid), there),
            pl.BlockSpec((1, hid, d), there),
        ]
        + [pl.BlockSpec(memory_space=pl.ANY) for _ in before],
        out_specs=[
            pl.BlockSpec((1, sub, hid), here),
            pl.BlockSpec((1, sub, hid), here),
            pl.BlockSpec((1, sub, d), here),
        ],
        out_shape=[wide, wide, jax.ShapeDtypeStruct((local, rows, d), BF16)],
        input_output_aliases={3 + k: k for k in range(len(before))},
        **params(4 * rows * d * hid * count, "forward"),
    )(shared, up, down, *before)


def same_row(n, m, group):
    row = lax.broadcasted_iota(jnp.int32, (n, m), 0) & (group - 1)
    lane = lax.broadcasted_iota(jnp.int32, (1, m), 1) & (group - 1)
    return jnp.where(row == lane, 1.0, 0.0)


def chosen(ids_ref, order, by_task, tasks, local, experts, cols, group):
    wide = tasks * local * group
    lane = shift(lax.broadcasted_iota(jnp.int32, (1, wide), 1), group)
    task = shift(lane, local) if by_task else lane & (tasks - 1)
    expert = lane & (local - 1) if by_task else shift(lane, tasks)
    ids = jnp.zeros_like(lane) + ids_ref[order]
    for t in range(1, tasks):
        ids = jnp.where(task == t, ids_ref[order + t], ids)
    row = lax.broadcasted_iota(jnp.int32, (cols, wide), 0)
    return jnp.where(row == ids * experts + ids_ref[0] + expert, 1.0, 0.0).astype(BF16)


def stack(weights, r, group, count, width):
    return jnp.concatenate(
        [weights[r : r + group, j * width : (j + 1) * width] for j in range(count)], axis=0
    )


def mix_kernel(tasks, experts, block, begin, ids_ref, gates_ref, outs_ref, mixed_ref):
    rows, cols = gates_ref.shape
    local = outs_ref.shape[0]
    group = 256 // local
    flat = same_row(block, tasks * local * group, group)
    step = rows // block
    for k in range(step):
        at = pl.ds(k * block, block)
        order = 1 + 2 * tasks * ((begin + pl.program_id(0)) * step + k) + tasks
        weights = mm(
            gates_ref[at, :].astype(BF16),
            chosen(ids_ref, order, True, tasks, local, experts, cols, group),
        )
        weights = (weights * flat).astype(BF16)
        for r in range(0, block, group):
            part = pl.ds(k * block + r, group)
            out = jnp.concatenate([outs_ref[j, part, :] for j in range(local)], axis=0)
            both = mm(stack(weights, r, group, tasks, local * group), out).astype(BF16)
            for t in range(tasks):
                mixed_ref[t, part, :] = both[t * group : (t + 1) * group]


def mix(ids, gates, outs, n, tasks):
    local, rows, d = outs.shape
    cols = gates.shape[1]
    sub = rows // 4

    def half(begin):
        return pl.pallas_call(
            functools.partial(mix_kernel, tasks, cols // tasks, rows // n, begin),
            grid_spec=pltpu.PrefetchScalarGridSpec(
                num_scalar_prefetch=1,
                grid=(2,),
                in_specs=[
                    pl.BlockSpec((sub, cols), lambda i, f: (begin + i, 0)),
                    pl.BlockSpec((local, sub, d), lambda i, f: (0, begin + i, 0)),
                ],
                out_specs=pl.BlockSpec((tasks, sub, d), lambda i, f: (0, i, 0)),
            ),
            out_shape=jax.ShapeDtypeStruct((tasks, rows // 2, d), BF16),
            **params(2**10 * rows * d, "mix"),
        )(ids, gates, outs)

    send = half(2)
    return half(0), send


def spread_kernel(tasks, experts, places, n_grads, ids_ref, *refs):
    grads = refs[:n_grads]
    gates_ref, outs_ref, og_ref, pair_ref, rows_ref, sems = refs[n_grads:]
    i = pl.program_id(0)
    rows, cols = gates_ref.shape
    count = rows_ref.shape[1]
    block = rows // count
    local = og_ref.shape[0]
    group = 256 // local

    def fetch(step, slot, act):
        for k in range(len(places) // count):

            @pl.when(step == k)
            def _():
                for j in range(count):
                    for t, (which, *lead) in enumerate(places[k * count + j]):
                        act(
                            pltpu.make_async_copy(
                                grads[which].at[tuple(lead)],
                                rows_ref.at[slot, j, t],
                                sems.at[slot, j, t],
                            )
                        )

    @pl.when(i == 0)
    def _():
        fetch(0, 0, lambda copy: copy.start())

    fetch(i + 1, (i + 1) & 1, lambda copy: copy.start())
    flat = same_row(block, tasks * local * group, group)
    square = same_row(tasks * group, local * group, group)
    fetch(i, i & 1, lambda copy: copy.wait())
    slot = i & 1
    for k in range(count):
        order = 1 + 2 * tasks * (i * count + k)
        at = pl.ds(k * block, block)
        gates = gates_ref[at, :]
        pick = lambda by_task: chosen(
            ids_ref, order, by_task, tasks, local, experts, cols, group
        )
        weights = (mm(gates.astype(BF16), pick(False)) * flat).astype(BF16)
        inners = []
        for r in range(0, block, group):
            part = pl.ds(k * block + r, group)
            grad = jnp.concatenate(
                [rows_ref[slot, k, t, r : r + group, :] for t in range(tasks)], axis=0
            )
            out = jnp.concatenate([outs_ref[j, part, :] for j in range(local)], axis=0)
            both = mm(stack(weights, r, group, local, tasks * group), grad).astype(BF16)
            for j in range(local):
                og_ref[j, part, :] = both[j * group : (j + 1) * group]
            products = mm(grad, out, NT) * square
            inners.append(
                jnp.concatenate(
                    [products[t * group : (t + 1) * group] for t in range(tasks)], axis=1
                )
            )
        inner = jnp.concatenate(inners, axis=0)
        high = inner.astype(BF16)
        rest = (inner - high.astype(F32)).astype(BF16)
        at_column = pick(True)
        inner = mm(high, at_column, NT) + mm(rest, at_column, NT)
        logit = gates * (inner - group_sum(gates * inner, experts))
        high = logit.astype(BF16)
        rest = (logit - high.astype(F32)).astype(BF16)
        row = lax.broadcasted_iota(jnp.int32, (cols, 2 * cols), 0)
        lane = lax.broadcasted_iota(jnp.int32, (cols, 2 * cols), 1)
        one = jnp.where(lane == row, 1.0, 0.0).astype(BF16)
        two = jnp.where(lane == row + cols, 1.0, 0.0).astype(BF16)
        pair_ref[at, :] = (mm(high, one) + mm(rest, two)).astype(BF16)


def spread_grads(ids, grads, places, gates, outs, tasks):
    local, rows, d = outs.shape
    cols = gates.shape[1]
    n = len(places)
    count = 2
    block = rows // n
    sub = count * block
    every = lambda i, f: (0, i, 0)
    return pl.pallas_call(
        functools.partial(spread_kernel, tasks, cols // tasks, places, len(grads)),
        grid_spec=pltpu.PrefetchScalarGridSpec(
            num_scalar_prefetch=1,
            grid=(n // count,),
            in_specs=[pl.BlockSpec(memory_space=pl.ANY) for _ in grads]
            + [
                pl.BlockSpec((sub, cols), lambda i, f: (i, 0)),
                pl.BlockSpec((local, sub, d), every),
            ],
            out_specs=[
                pl.BlockSpec((local, sub, d), every),
                pl.BlockSpec((sub, 2 * cols), lambda i, f: (i, 0)),
            ],
            scratch_shapes=[
                pltpu.VMEM((2, count, tasks, block, d), BF16),
                pltpu.SemaphoreType.DMA((2, count, tasks)),
            ],
        ),
        out_shape=[
            jax.ShapeDtypeStruct((local, rows, d), BF16),
            jax.ShapeDtypeStruct((rows, 2 * cols), BF16),
        ],
        **params(2**11 * rows * d, "spread_grads"),
    )(ids, *grads, gates, outs)


def backward_kernel(
    tasks, n, sub,
    ids_ref, og_ref, slope_ref, up_ref, down_ref, pair_ref, pg_ref, keep_ref, send_ref, acc_ref,
):
    e = pl.program_id(0)
    rows, d = acc_ref.shape
    for r in range(0, rows, sub):
        part = pl.ds(r, sub)
        hidden = mm(og_ref[0, part, :], down_ref[0], NT)
        pre_grad = (hidden * slope_ref[0, part, :].astype(F32)).astype(BF16)
        pg_ref[0, part, :] = pre_grad
        found = mm(pre_grad, up_ref[0], NT)

        @pl.when(e == 0)
        def _():
            acc_ref[part, :] = found

        @pl.when(e > 0)
        def _():
            acc_ref[part, :] += found

    block = rows // n
    quarter = block // tasks

    @pl.when(e == pl.num_programs(0) - 1)
    def _():
        for i in range(n):
            ref = keep_ref if i < n // 2 else send_ref
            for t in range(tasks):
                place = ids_ref[1 + 2 * tasks * i + tasks + t]
                begin = pl.multiple_of(i * block + place * quarter, quarter)
                source = pl.ds(begin, quarter)
                dest = pl.ds(i % (n // 2) * quarter, quarter)
                ref[t, dest, :d] = acc_ref[source, :].astype(BF16)
                ref[t, dest, d:] = pair_ref[source, :]


def backward(ids, og, slope, up, down, pair, n, tasks):
    local, rows, d = og.shape
    hid = up.shape[2]
    here = lambda e, f: (e, 0, 0)
    width = d + pair.shape[1]
    packed = (tasks, rows // 2 // tasks, width)
    return pl.pallas_call(
        functools.partial(backward_kernel, tasks, n, min(rows, 512)),
        grid_spec=pltpu.PrefetchScalarGridSpec(
            num_scalar_prefetch=1,
            grid=(local,),
            in_specs=[
                pl.BlockSpec((1, rows, d), here),
                pl.BlockSpec((1, rows, hid), here),
                pl.BlockSpec((1, d, hid), here),
                pl.BlockSpec((1, hid, d), here),
                pl.BlockSpec(pair.shape, lambda e, f: (0, 0)),
            ],
            out_specs=[pl.BlockSpec((1, rows, hid), here)]
            + [pl.BlockSpec(packed, lambda e, f: (0, 0, 0))] * 2,
            scratch_shapes=[pltpu.VMEM((rows, d), F32)],
        ),
        out_shape=[jax.ShapeDtypeStruct((local, rows, hid), BF16)]
        + [jax.ShapeDtypeStruct(packed, BF16)] * 2,
        **params(4 * rows * d * hid * local, "backward"),
    )(ids, og, slope, up, down, pair)


def weights_kernel(n, *refs):
    shared, acts, ogs, pgs = (refs[k * n : (k + 1) * n] for k in range(4))
    up_ref, down_ref = refs[-2:]
    total = sum(mm(s[...], p[0], TN) for s, p in zip(shared, pgs))
    up_ref[0] = total.astype(BF16)
    total = sum(mm(a[0], o[0], TN) for a, o in zip(acts, ogs))
    down_ref[0] = total.astype(BF16)


def weight_grads(shared, acts, ogs, pgs, begin, count, before):
    local, rows, hid = acts[0].shape
    d = shared[0].shape[1]
    n = len(shared)
    there = lambda e, h: (begin + e, 0, 0)
    half = [pl.BlockSpec((1, x.shape[1], hid // 2), lambda e, h: (begin + e, 0, h)) for x in acts]
    return pl.pallas_call(
        functools.partial(weights_kernel, n),
        grid=(count, 2),
        in_specs=[pl.BlockSpec(s.shape, lambda e, h: (0, 0)) for s in shared]
        + half
        + [pl.BlockSpec((1,) + x.shape[1:], there) for x in ogs]
        + half
        + [pl.BlockSpec(memory_space=pl.ANY) for _ in before],
        out_specs=[
            pl.BlockSpec((1, d, hid // 2), lambda e, h: (begin + e, 0, h)),
            pl.BlockSpec((1, hid // 2, d), lambda e, h: (begin + e, h, 0)),
        ],
        out_shape=[
            jax.ShapeDtypeStruct((local, d, hid), BF16),
            jax.ShapeDtypeStruct((local, hid, d), BF16),
        ],
        input_output_aliases={4 * n + k: k for k in range(len(before))},
        **params(4 * n * rows * d * hid * count, "weight_grads"),
    )(*shared, *acts, *ogs, *pgs, *before)


def rows_kernel(cols, every_ref, feat_ref, shared_ref, cross_ref, bias_ref, gating_ref, offset_ref):
    i = pl.program_id(0)
    d = feat_ref.shape[1]

    @pl.when(i == 0)
    def _():
        for ref in (cross_ref, bias_ref, gating_ref, offset_ref):
            ref[...] = jnp.zeros_like(ref)

    scaled = (every_ref[:, :d].astype(F32) * feat_ref[...].astype(F32)).astype(BF16)
    cross_ref[...] += mm(feat_ref[...], scaled, TN)
    bias_ref[...] += jnp.sum(scaled.astype(F32), axis=0, keepdims=True)
    pair = every_ref[:, d:]
    gating_ref[...] += mm(shared_ref[...], pair, TN)
    offset_ref[...] += jnp.sum(pair.astype(F32), axis=0, keepdims=True)


def rows_grads(every, feat, shared, cols):
    rows, d = feat.shape
    sub = min(rows, 512)
    width = every.shape[1]
    whole = lambda i: (0, 0)
    cross_grad, bias, gating, offset = pl.pallas_call(
        functools.partial(rows_kernel, cols),
        grid=(rows // sub,),
        in_specs=[
            pl.BlockSpec((sub, width), lambda i: (i, 0)),
            pl.BlockSpec((sub, d), lambda i: (i, 0)),
            pl.BlockSpec((sub, d), lambda i: (i, 0)),
        ],
        out_specs=[
            pl.BlockSpec((d, d), whole),
            pl.BlockSpec((1, d), whole),
            pl.BlockSpec((d, width - d), whole),
            pl.BlockSpec((1, width - d), whole),
        ],
        out_shape=[
            jax.ShapeDtypeStruct((d, d), F32),
            jax.ShapeDtypeStruct((1, d), F32),
            jax.ShapeDtypeStruct((d, width - d), F32),
            jax.ShapeDtypeStruct((1, width - d), F32),
        ],
        **params(2 * rows * d * d, "rows_grads"),
    )(every, feat, shared)
    return cross_grad, bias, gating[:, :cols], offset[0, :cols] + offset[0, cols:]


def added(parts):
    return sum(p.astype(F32) for p in parts)


class Ring:
    def __init__(self, dp, expert):
        size = dp * expert

        def pairs(move):
            found = []
            for i in range(size):
                z, c, q = i // expert // 2, i // expert % 2, i % expert
                z, c, q = move(z, c, q)
                found.append((i, (z * 2 + c) * expert + q))
            return found

        self.core_pairs = pairs(lambda z, c, q: (z, 1 - c, q))
        self.z1_pairs = pairs(lambda z, c, q: (z ^ 1, c, q))
        self.z3_pairs = pairs(lambda z, c, q: (z ^ 3, c, q))
        self.e1_pairs = pairs(lambda z, c, q: (z, c, q ^ (1, 2)[c]))
        self.e2_pairs = pairs(lambda z, c, q: (z, c, q ^ (2, 1)[c]))

    def move(self, x, pairs):
        return lax.ppermute(x, ("dp", "expert"), pairs)

    def core(self, x):
        return self.move(x, self.core_pairs)

    def orders(self):
        q, c = lax.axis_index("expert"), lax.axis_index("dp") % 2
        b1, b2 = 1 + c, 2 - c
        return [q, q ^ b2, q ^ b1, q ^ 3], [q, q ^ b1, q ^ b2, q ^ 3]

    def ids(self, first, tasks):
        mine, other = self.orders()
        plain = list(range(tasks))
        ids = [first]
        for order in (mine, other):
            for k in range(4):
                ids += plain if k == 0 else (other if order is mine else mine)
                ids += order
        return [jnp.stack([jnp.asarray(i, jnp.int32) for i in ids])]

    def spread(self, x):
        one = self.move(x, self.e1_pairs)
        rest = self.move(jnp.stack([x, one]), self.e2_pairs)
        return x[None], one[None], rest

    def in_order(self, parts, order):
        parts = jnp.concatenate(parts, axis=0)
        place = lambda share: sum(jnp.where(order[i] == share, i, 0) for i in range(4))
        return [lax.dynamic_index_in_dim(parts, place(i), 0, False) for i in range(4)]

    def rows(self, x):
        three = self.move(x, self.z3_pairs)
        mine = jnp.stack([x, three])
        rest = self.move(mine, self.z1_pairs)
        mine = jnp.concatenate([mine, rest], axis=0).reshape(-1, x.shape[-1])
        return [jnp.concatenate([mine, self.core(mine)], axis=0)], three, rest

    def grads(self, task_grad):
        own = jnp.transpose(task_grad, (1, 0, 2))
        share = lax.dynamic_index_in_dim(task_grad, lax.axis_index("expert"), 1, False)
        core, move = self.core, self.move
        share, own = yield (share, own)
        three, own2 = yield (move(share, self.z3_pairs), core(own))
        a0 = three[None]
        both, a0 = yield (jnp.stack([share, three]), a0)
        b0, a1 = yield (move(both, self.z1_pairs), move(a0, self.e1_pairs))
        b0, out = yield (b0, jnp.stack([a0, a1]))
        b1, a2 = yield (move(b0, self.e1_pairs), move(out, self.e2_pairs))
        out, *a = yield (jnp.stack([b0, b1]), a0, a1, a2)
        b2, *other_a = yield (move(out, self.e2_pairs), *map(core, a))
        b = yield (b0, b1, b2)
        other_b = yield tuple(map(core, b))
        lift = lambda x, y, z: [x[None], y[None], z]
        refs = [own, *lift(*a), *lift(*b), own2, *lift(*other_a), *lift(*other_b)]
        places = []
        for w in (0, 7):
            places.append(tuple((w, t) for t in range(4)))
            for k, j in ((1, 0), (4, 0), (4, 1)):
                places.append(
                    ((w + k, 0, j), (w + k + 1, 0, j), (w + k + 2, 0, j), (w + k + 2, 1, j))
                )
        return [(refs, tuple(places))]

    def reduce(self, parts, scatter):
        ((keep, send),) = parts
        (out,) = yield (send,)
        (got,) = yield (self.core(out),)
        parts = [keep, got]
        (out,) = yield (added([p[2:] for p in parts]).astype(BF16),)
        (got,) = yield (self.move(out, self.e1_pairs),)
        parts = [p[:2] for p in parts] + [got]
        (out,) = yield (added([p[1] for p in parts]).astype(BF16),)
        (got,) = yield (self.move(out, self.e2_pairs),)
        parts = [p[0] for p in parts] + [got]
        half = got.shape[0] // 2
        if scatter:
            (out,) = yield (added([p[half:] for p in parts]).astype(BF16),)
            (got,) = yield (self.move(out, self.z1_pairs),)
            parts = [p[:half] for p in parts] + [got]
            half = half // 2
            (out,) = yield (added([p[half:] for p in parts]).astype(BF16),)
            (got,) = yield (self.move(out, self.z3_pairs),)
            return added([p[:half] for p in parts] + [got])
        shape = (4, -1, got.shape[-1])
        (out,) = yield (added(parts).astype(BF16).reshape(shape),)
        (got,) = yield (self.move(out, self.z1_pairs),)
        out = added([out, jnp.concatenate([got[2:], got[:2]], axis=0)])
        (out,) = yield (out.astype(BF16),)
        (got,) = yield (self.move(out, self.z3_pairs),)
        return added([out, jnp.stack([got[1], got[0], got[3], got[2]])])

    def share_tasks(self, x):
        return self.in_order(self.spread(x), self.orders()[1])

    def share_rows(self, x):
        mine = self.spread(x)
        other = [self.core(p) for p in mine]
        rows = []
        for parts, order in zip((mine, other), self.orders()[::-1]):
            rows.append(jnp.stack(self.in_order(parts, order), axis=1).reshape(-1, x.shape[-1]))
        return jnp.concatenate(rows, axis=0)

    def own_rows(self, rows):
        return rows[: rows.shape[0] // 8]


class Steps:
    def __init__(self, steps):
        self.steps, self.moved, self.value = steps, None, None
        self.operand = self._next(None)

    def _next(self, sent):
        try:
            return self.steps.send(sent)
        except StopIteration as stop:
            self.value = stop.value

    def start(self, *after):
        if self.operand is not None:
            self.moved, self.operand = self._next(tie(self.operand, *after)), None

    def finish(self, *after):
        if self.moved is not None:
            moved, self.moved = self.moved, None
            self.operand = self._next(tie(moved, *after))

    def result(self):
        while self.moved is not None or self.operand is not None:
            self.start()
            self.finish()
        return self.value


def tie(x, *others):
    others = [o for o in others if o is not None]
    return lax.optimization_barrier((x, *others))[0] if others else x


class Plain:
    def __init__(self, dp, expert):
        self.dp = dp
        self.count = dp // 8 if dp % 8 == 0 else 1
        self.blocks = dp // self.count

    def ids(self, first, tasks):
        plain = list(range(tasks)) * 2 * self.blocks
        return [jnp.stack([jnp.asarray(i, jnp.int32) for i in (first, *plain)])] * self.count

    def rows(self, x):
        every = lax.all_gather(x, "dp", axis=0, tiled=True)
        return jnp.split(every, self.count), None, None

    def grads(self, task_grad):
        every = lax.all_gather(jnp.transpose(task_grad, (1, 0, 2)), "dp", axis=0)
        tasks = task_grad.shape[1]
        places = tuple(tuple((0, i, t) for t in range(tasks)) for i in range(self.blocks))
        return [([part], places) for part in jnp.split(every, self.count)]
        yield

    def reduce(self, parts, scatter):
        blocks = []
        for part in (p for pair in parts for p in pair):
            part = part.reshape(part.shape[0], self.blocks // 2, -1, part.shape[-1])
            blocks.append(jnp.swapaxes(part.astype(F32), 0, 1))
        blocks = jnp.concatenate(blocks, axis=0)
        own = lax.psum_scatter(blocks, "dp", scatter_dimension=0, tiled=True)[0]
        return lax.psum(own, "expert")
        yield

    def share_tasks(self, x):
        return list(x)

    def share_rows(self, x):
        every = lax.all_gather(x, "dp", axis=0)
        return every.reshape(-1, x.shape[-1])

    def own_rows(self, rows):
        n = rows.shape[0] // self.dp
        return lax.dynamic_slice_in_dim(rows, lax.axis_index("dp") * n, n, 0)


def local_step(
    net, features, cross_weight, cross_bias, gate_weight, gate_offset, up_weight, down_weight,
    task_grad,
):
    block, d = features.shape
    tasks = task_grad.shape[1]
    cols = gate_weight.shape[1]
    local = up_weight.shape[0]
    first = lax.axis_index("expert") * local
    ids = net.ids(first, tasks)
    step = max(local // FORWARD_PARTS, 1)

    feats, early, late = net.rows(features)
    grads = Steps(net.grads(task_grad))
    grads.start(early)

    lowered = [
        cross(f, cross_weight[0], cross_bias, gate_weight, gate_offset[None], tasks)
        for f in feats
    ]
    shared, gates = zip(*lowered)
    grads.finish(*shared)
    ready = grads.operand
    grads.start()
    done = [() for _ in shared]
    for b in range(0, local, step):
        if b:
            grads.finish(*[found[0] for found in done])
            ready = grads.operand
            grads.start()
        done = [
            forward(tie(low, ready), up_weight, down_weight, b, step, found)
            for low, found in zip(shared, done)
        ]
    acts, slopes, outs = zip(*done)
    grads.finish()
    grads = grads.result()
    lowered = [tie(gt, *g[0]) for gt, g in zip(gates, grads)]
    mixed = [mix(i, gt, o, len(g[1]), tasks) for i, gt, o, g in zip(ids, lowered, outs, grads)]
    mixed = Steps(net.reduce(mixed, True))
    mixed.start()
    spread = [
        spread_grads(i, *g, gt, o, tasks) for i, g, gt, o in zip(ids, grads, gates, outs)
    ]
    mixed.finish(*[og for og, _ in spread])
    ready = mixed.operand
    mixed.start()
    back = [
        backward(i, tie(og, ready), slope, up_weight, down_weight, pair, len(g[1]), tasks)
        for i, (og, pair), slope, g in zip(ids, spread, slopes, grads)
    ]
    ogs = [og for og, _ in spread]
    pgs = [b[0] for b in back]
    total = Steps(net.reduce([b[1:] for b in back], False))
    total.start()
    total.finish()
    mixed.finish(*pgs)
    weights = ()
    step = max(local // WEIGHT_PARTS, 1)
    for b in range(0, local, step):
        ready = (mixed.operand, total.operand)
        total.start()
        mixed.start()
        tied = [tie(a, *ready) for a in acts]
        weights = weight_grads(shared, tied, ogs, pgs, b, step, weights)
        total.finish(weights[0])
        mixed.finish(weights[0])
        total.start()
        total.finish()
    up_grad, down_grad = weights
    total = total.result()
    task_mixed = mixed.result().astype(BF16)
    task_mixed = jnp.stack(net.share_tasks(task_mixed), axis=1)

    logit = total[..., d : d + cols] + total[..., d + cols :]
    high = logit.astype(BF16)
    low = (logit - high.astype(F32)).astype(BF16)
    upstream = total[..., :d] + lax.dot_general(
        high, gate_weight, (((high.ndim - 1,), (1,)), ((), ())), preferred_element_type=F32
    )
    every = net.share_rows(jnp.concatenate([upstream.astype(BF16), high, low], axis=-1))

    cross_grad, bias_grad, gating_grad, offset_grad = rows_grads(
        every, jnp.concatenate(feats, axis=0), jnp.concatenate(shared, axis=0), cols
    )

    update = mm(features, cross_weight[0]) + cross_bias
    upstream = net.own_rows(every[:, :d]).astype(F32)
    scaled = (upstream * features.astype(F32)).astype(BF16)
    feature_grad = (upstream + mm(scaled, cross_weight[0], NT) + upstream * update).astype(BF16)
    return (
        task_mixed,
        feature_grad,
        up_grad,
        down_grad,
        cross_grad[None],
        bias_grad,
        gating_grad,
        offset_grad,
    )


def solution(mesh):
    dp, expert = mesh.shape["dp"], mesh.shape["expert"]
    net = (Ring if (dp, expert) == (8, 4) else Plain)(dp, expert)
    return jax.shard_map(
        functools.partial(local_step, net),
        mesh=mesh,
        in_specs=(
            P("dp", None),
            P(),
            P(),
            P(),
            P(),
            P("expert", None, "dp"),
            P("expert", "dp", None),
            P("dp", None, None),
        ),
        out_specs=(
            P("dp", None, None),
            P("dp", None),
            P("expert", None, "dp"),
            P("expert", "dp", None),
            P(),
            P(),
            P(),
            P(),
        ),
        check_vma=False,
    )
```

```python
import functools
import itertools

import jax
import jax.numpy as jnp
from jax import lax
from jax.experimental import pallas as pl
from jax.experimental.pallas import tpu as pltpu
from jax.sharding import PartitionSpec as P

F32 = jnp.float32
BF16 = jnp.bfloat16
NN = (((1,), (0,)), ((), ()))
NT = (((1,), (1,)), ((), ()))
TN = (((0,), (0,)), ((), ()))
VMEM_LIMIT = 56 * 2**20
BACKWARD_PARTS = 1


def mm(a, b, dims=NN):
    return lax.dot_general(a, b, dims, preferred_element_type=F32)


def exact(values, ones):
    high = values.astype(BF16)
    low = (values - high.astype(F32)).astype(BF16)
    return mm(high, ones) + mm(low, ones)


def shift(values, size):
    assert size & (size - 1) == 0
    return lax.shift_right_logical(values, jnp.int32(size.bit_length() - 1))


def group_sum(values, experts):
    n = values.shape[1]
    row = shift(lax.broadcasted_iota(jnp.int32, (n, n), 0), experts)
    lane = shift(lax.broadcasted_iota(jnp.int32, (n, n), 1), experts)
    return exact(values, jnp.where(row == lane, 1.0, 0.0).astype(BF16))


def params(flops, name):
    return dict(
        compiler_params=pltpu.CompilerParams(vmem_limit_bytes=VMEM_LIMIT),
        cost_estimate=pl.CostEstimate(flops=flops, bytes_accessed=2**24, transcendentals=0),
        name=name,
    )


def cross_kernel(experts, n, *refs):
    feats, (cw_ref, cb_ref, gw_ref, go_ref) = refs[: 2 * n], refs[2 * n : 2 * n + 4]
    every_ref, shared_ref, gates_ref = refs[-3:]
    block = feats[0].shape[0]

    def half(feats):
        base = jnp.concatenate([f[...] for f in feats], axis=0)
        part = pl.ds(0, n * block)
        every_ref[part, :] = base
        wide = base.astype(F32)
        update = mm(base, cw_ref[...]) + cb_ref[...]
        shared = (wide * update + wide).astype(BF16)
        shared_ref[part, :] = shared
        expo = jnp.exp(mm(shared, gw_ref[...], NT) + go_ref[...])
        gates_ref[part, :] = expo / group_sum(expo, experts)

    pl.when(pl.program_id(0) == 0)(lambda: half(feats[:n]))
    pl.when(pl.program_id(0) == 1)(lambda: half(feats[n:]))


def cross(feats, cw, cb, gw, go, blocks, begin, before, tasks):
    block, d = feats[0].shape
    n = len(feats) // 2
    rows = 2 * blocks * block
    cols = gw.shape[0]
    vmem = pl.BlockSpec(memory_space=pltpu.VMEM)
    size = blocks if begin == 0 else n
    place = lambda i: ((i * blocks + begin) // size, 0)
    return pl.pallas_call(
        functools.partial(cross_kernel, cols // tasks, n),
        grid=(2,),
        in_specs=[vmem] * (len(feats) + 4) + [pl.BlockSpec(memory_space=pl.ANY) for _ in before],
        out_specs=[
            pl.BlockSpec((size * block, d), place),
            pl.BlockSpec((size * block, d), place),
            pl.BlockSpec((size * block, cols), place),
        ],
        out_shape=[
            jax.ShapeDtypeStruct((rows, d), BF16),
            jax.ShapeDtypeStruct((rows, d), BF16),
            jax.ShapeDtypeStruct((rows, cols), F32),
        ],
        input_output_aliases={len(feats) + 4 + k: k for k in range(len(before))},
        **params(n * 4 * block * d * d, "cross"),
    )(*feats, cw, cb, gw, go, *before)


def forward_kernel(shared_ref, up_ref, down_ref, *refs):
    act_ref, slope_ref, out_ref = refs[-3:]
    pre = mm(shared_ref[...], up_ref[0])
    sig = jax.nn.sigmoid(pre)
    act = pre * sig
    low = act.astype(BF16)
    act_ref[0] = low
    slope_ref[0] = (sig + act * (1.0 - sig)).astype(BF16)
    out_ref[0] = mm(low, down_ref[0]).astype(BF16)


def forward(shared, up, down, begin, count, before):
    rows, d = shared.shape
    local, _, hid = up.shape
    sub = min(rows, 512)
    here = lambda e, r: (begin + e, r, 0)
    there = lambda e, r: (begin + e, 0, 0)
    wide = jax.ShapeDtypeStruct((local, rows, hid), BF16)
    return pl.pallas_call(
        forward_kernel,
        grid=(count, rows // sub),
        in_specs=[
            pl.BlockSpec((sub, d), lambda e, r: (r, 0)),
            pl.BlockSpec((1, d, hid), there),
            pl.BlockSpec((1, hid, d), there),
        ]
        + [pl.BlockSpec(memory_space=pl.ANY) for _ in before],
        out_specs=[
            pl.BlockSpec((1, sub, hid), here),
            pl.BlockSpec((1, sub, hid), here),
            pl.BlockSpec((1, sub, d), here),
        ],
        out_shape=[wide, wide, jax.ShapeDtypeStruct((local, rows, d), BF16)],
        input_output_aliases={3 + k: k for k in range(len(before))},
        **params(4 * rows * d * hid * count, "forward"),
    )(shared, up, down, *before)


def same_row(n, m, group):
    row = lax.broadcasted_iota(jnp.int32, (n, m), 0) & (group - 1)
    lane = lax.broadcasted_iota(jnp.int32, (1, m), 1) & (group - 1)
    return jnp.where(row == lane, 1.0, 0.0)


def chosen(ids_ref, order, by_task, tasks, local, experts, cols, group):
    wide = tasks * local * group
    lane = shift(lax.broadcasted_iota(jnp.int32, (1, wide), 1), group)
    task = shift(lane, local) if by_task else lane & (tasks - 1)
    expert = lane & (local - 1) if by_task else shift(lane, tasks)
    ids = jnp.zeros_like(lane) + ids_ref[order]
    for t in range(1, tasks):
        ids = jnp.where(task == t, ids_ref[order + t], ids)
    row = lax.broadcasted_iota(jnp.int32, (cols, wide), 0)
    return jnp.where(row == ids * experts + ids_ref[0] + expert, 1.0, 0.0).astype(BF16)


def stack(weights, r, group, count, width):
    return jnp.concatenate(
        [weights[r : r + group, j * width : (j + 1) * width] for j in range(count)], axis=0
    )


def mix_kernel(tasks, experts, block, ids_ref, gates_ref, outs_ref, keep_ref, send_ref):
    i = pl.program_id(0)
    rows, cols = gates_ref.shape
    local = outs_ref.shape[0]
    group = 256 // local
    flat = same_row(block, tasks * local * group, group)
    step = rows // block

    def write(ref):
        for k in range(step):
            at = pl.ds(k * block, block)
            order = 1 + 2 * tasks * (i * step + k) + tasks
            weights = mm(
                gates_ref[at, :].astype(BF16),
                chosen(ids_ref, order, True, tasks, local, experts, cols, group),
            )
            weights = (weights * flat).astype(BF16)
            for r in range(0, block, group):
                part = pl.ds(k * block + r, group)
                out = jnp.concatenate([outs_ref[j, part, :] for j in range(local)], axis=0)
                both = mm(stack(weights, r, group, tasks, local * group), out).astype(BF16)
                for t in range(tasks):
                    ref[t, part, :] = both[t * group : (t + 1) * group]

    pl.when(i < pl.num_programs(0) // 2)(lambda: write(keep_ref))
    pl.when(i >= pl.num_programs(0) // 2)(lambda: write(send_ref))


def mix(ids, gates, outs, n, tasks):
    local, rows, d = outs.shape
    cols = gates.shape[1]
    sub = rows // 4
    return pl.pallas_call(
        functools.partial(mix_kernel, tasks, cols // tasks, rows // n),
        grid_spec=pltpu.PrefetchScalarGridSpec(
            num_scalar_prefetch=1,
            grid=(4,),
            in_specs=[
                pl.BlockSpec((sub, cols), lambda i, f: (i, 0)),
                pl.BlockSpec((local, sub, d), lambda i, f: (0, i, 0)),
            ],
            out_specs=[
                pl.BlockSpec((tasks, sub, d), lambda i, f: (0, jnp.minimum(i, 1), 0)),
                pl.BlockSpec((tasks, sub, d), lambda i, f: (0, jnp.maximum(i - 2, 0), 0)),
            ],
        ),
        out_shape=[jax.ShapeDtypeStruct((tasks, rows // 2, d), BF16)] * 2,
        **params(2**11 * rows * d, "mix"),
    )(ids, gates, outs)


def spread_kernel(tasks, experts, places, n_grads, begin, ids_ref, *refs):
    grads = refs[:n_grads]
    gates_ref, outs_ref = refs[n_grads : n_grads + 2]
    og_ref, inner_ref, rows_ref, sems = refs[-4:]
    i = pl.program_id(0)
    rows, cols = gates_ref.shape
    count = rows_ref.shape[1]
    block = rows // count
    local = og_ref.shape[0]
    group = 256 // local

    def fetch(step, slot, act):
        for k in range(len(places) // count):

            @pl.when(step == k)
            def _():
                for j in range(count):
                    for t, (which, *lead) in enumerate(places[k * count + j]):
                        act(
                            pltpu.make_async_copy(
                                grads[which].at[tuple(lead)],
                                rows_ref.at[slot, j, t],
                                sems.at[slot, j, t],
                            )
                        )

    @pl.when(i == 0)
    def _():
        fetch(0, 0, lambda copy: copy.start())

    fetch(i + 1, (i + 1) & 1, lambda copy: copy.start())
    flat = same_row(block, tasks * local * group, group)
    square = same_row(tasks * group, local * group, group)
    fetch(i, i & 1, lambda copy: copy.wait())
    slot = i & 1
    for k in range(count):
        order = 1 + 2 * tasks * ((begin + i) * count + k)
        at = pl.ds(k * block, block)
        gates = gates_ref[at, :]
        pick = lambda by_task: chosen(
            ids_ref, order, by_task, tasks, local, experts, cols, group
        )
        weights = (mm(gates.astype(BF16), pick(False)) * flat).astype(BF16)
        inners = []
        for r in range(0, block, group):
            part = pl.ds(k * block + r, group)
            grad = jnp.concatenate(
                [rows_ref[slot, k, t, r : r + group, :] for t in range(tasks)], axis=0
            )
            out = jnp.concatenate([outs_ref[j, part, :] for j in range(local)], axis=0)
            both = mm(stack(weights, r, group, local, tasks * group), grad).astype(BF16)
            for j in range(local):
                og_ref[j, part, :] = both[j * group : (j + 1) * group]
            products = mm(grad, out, NT) * square
            inners.append(
                jnp.concatenate(
                    [products[t * group : (t + 1) * group] for t in range(tasks)], axis=1
                )
            )
        inner = jnp.concatenate(inners, axis=0)
        high = inner.astype(BF16)
        rest = (inner - high.astype(F32)).astype(BF16)
        at_column = pick(True)
        inner_ref[at, :] = mm(high, at_column, NT) + mm(rest, at_column, NT)


def spread_grads(ids, grads, places, gates, outs, begin, before, tasks):
    local, rows, d = outs.shape
    cols = gates.shape[1]
    n = len(places)
    count = 2
    block = rows // 2 // n
    sub = count * block
    begin = begin * (n // count)
    every = lambda i, f: (0, begin + i, 0)
    here = lambda i, f: (begin + i, 0)
    return pl.pallas_call(
        functools.partial(spread_kernel, tasks, cols // tasks, places, len(grads), begin),
        grid_spec=pltpu.PrefetchScalarGridSpec(
            num_scalar_prefetch=1,
            grid=(n // count,),
            in_specs=[pl.BlockSpec(memory_space=pl.ANY) for _ in grads]
            + [pl.BlockSpec((sub, cols), here), pl.BlockSpec((local, sub, d), every)]
            + [pl.BlockSpec(memory_space=pl.ANY) for _ in before],
            out_specs=[
                pl.BlockSpec((local, sub, d), every),
                pl.BlockSpec((sub, cols), here),
            ],
            scratch_shapes=[
                pltpu.VMEM((2, count, tasks, block, d), BF16),
                pltpu.SemaphoreType.DMA((2, count, tasks)),
            ],
        ),
        out_shape=[
            jax.ShapeDtypeStruct((local, rows, d), BF16),
            jax.ShapeDtypeStruct((rows, cols), F32),
        ],
        input_output_aliases={3 + len(grads) + k: k for k in range(len(before))},
        **params(2**10 * rows * d, "spread_grads"),
    )(ids, *grads, gates, outs, *before)


def backward_kernel(tasks, experts, n, sub, start, last, ids_ref, *refs):
    og_ref, slope_ref, up_ref, down_ref = refs[:4]
    total_ref = None if start else refs[4]
    if last:
        gates_ref, inner_ref = refs[5 - start : 7 - start]
        pg_ref, keep_ref, send_ref, acc_ref, pair_ref = refs[-5:]
    else:
        pg_ref, acc_ref = refs[-2:]
    e = pl.program_id(0)
    rows, d = acc_ref.shape

    for r in range(0, rows, sub):
        part = pl.ds(r, sub)
        hidden = mm(og_ref[0, part, :], down_ref[0], NT)
        pre_grad = (hidden * slope_ref[0, part, :].astype(F32)).astype(BF16)
        pg_ref[0, part, :] = pre_grad
        found = mm(pre_grad, up_ref[0], NT)

        @pl.when(e == 0)
        def _():
            acc_ref[part, :] = found if start else total_ref[part, :] + found

        @pl.when(e > 0)
        def _():
            acc_ref[part, :] += found

    if not last:
        return
    cols = gates_ref.shape[1]
    block = rows // n
    quarter = block // tasks

    @pl.when(e == 0)
    def _():
        gates, inner = gates_ref[...], inner_ref[...]
        logit = gates * (inner - group_sum(gates * inner, experts))
        high = logit.astype(BF16)
        rest = (logit - high.astype(F32)).astype(BF16)
        row = lax.broadcasted_iota(jnp.int32, (cols, 2 * cols), 0)
        lane = lax.broadcasted_iota(jnp.int32, (cols, 2 * cols), 1)
        one = jnp.where(lane == row, 1.0, 0.0).astype(BF16)
        two = jnp.where(lane == row + cols, 1.0, 0.0).astype(BF16)
        pair_ref[...] = (mm(high, one) + mm(rest, two)).astype(BF16)

    @pl.when(e == pl.num_programs(0) - 1)
    def _():
        for i in range(n):
            ref = keep_ref if i < n // 2 else send_ref
            for t in range(tasks):
                place = ids_ref[1 + 2 * tasks * i + tasks + t]
                begin = pl.multiple_of(i * block + place * quarter, quarter)
                source = pl.ds(begin, quarter)
                dest = pl.ds(i % (n // 2) * quarter, quarter)
                ref[t, dest, :d] = acc_ref[source, :].astype(BF16)
                ref[t, dest, d:] = pair_ref[source, :]


def backward(ids, og, slope, up, down, gates, inner, n, begin, count, before, last, tasks):
    local, rows, d = og.shape
    hid = up.shape[2]
    here = lambda e, f: (begin + e, 0, 0)
    cols = gates.shape[1]
    width = d + 2 * cols
    packed = (tasks, rows // 2 // tasks, width)
    start = before is None
    whole = lambda shape, **how: pl.BlockSpec(shape, lambda e, f: (0,) * len(shape), **how)
    specs, shapes, scratch = [whole((rows, d))], [jax.ShapeDtypeStruct((rows, d), F32)], []
    if last:
        specs, shapes = [whole(packed)] * 2, [jax.ShapeDtypeStruct(packed, BF16)] * 2
        scratch = [pltpu.VMEM((rows, d), F32), pltpu.VMEM((rows, 2 * cols), BF16)]
    args, in_specs = [], []
    if not start:
        args, in_specs = [before[1]], [whole((rows, d), pipeline_mode=pl.Buffered(1))]
    if last:
        args, in_specs = args + [gates, inner], in_specs + [whole((rows, cols))] * 2
    if not start:
        args, in_specs = args + [before[0]], in_specs + [pl.BlockSpec(memory_space=pl.ANY)]
    return pl.pallas_call(
        functools.partial(
            backward_kernel, tasks, cols // tasks, n, min(rows, 512), start, last
        ),
        grid_spec=pltpu.PrefetchScalarGridSpec(
            num_scalar_prefetch=1,
            grid=(count,),
            in_specs=[
                pl.BlockSpec((1, rows, d), here),
                pl.BlockSpec((1, rows, hid), here),
                pl.BlockSpec((1, d, hid), here),
                pl.BlockSpec((1, hid, d), here),
            ]
            + in_specs,
            out_specs=[pl.BlockSpec((1, rows, hid), here)] + specs,
            scratch_shapes=scratch,
        ),
        out_shape=[jax.ShapeDtypeStruct((local, rows, hid), BF16)] + shapes,
        input_output_aliases={} if start else {4 + len(args): 0},
        **params(4 * rows * d * hid * count, "backward"),
    )(ids, og, slope, up, down, *args)


def weights_kernel(n, *refs):
    shared, acts, ogs, pgs = (refs[k * n : (k + 1) * n] for k in range(4))
    up_ref, down_ref = refs[-2:]
    total = sum(mm(s[...], p[0], TN) for s, p in zip(shared, pgs))
    up_ref[0] = total.astype(BF16)
    total = sum(mm(a[0], o[0], TN) for a, o in zip(acts, ogs))
    down_ref[0] = total.astype(BF16)


def weight_grads(shared, acts, ogs, pgs, begin, count, before):
    local, rows, hid = acts[0].shape
    d = shared[0].shape[1]
    n = len(shared)
    there = lambda e, h: (begin + e, 0, 0)
    half = [pl.BlockSpec((1, x.shape[1], hid // 2), lambda e, h: (begin + e, 0, h)) for x in acts]
    return pl.pallas_call(
        functools.partial(weights_kernel, n),
        grid=(count, 2),
        in_specs=[pl.BlockSpec(s.shape, lambda e, h: (0, 0)) for s in shared]
        + half
        + [pl.BlockSpec((1,) + x.shape[1:], there) for x in ogs]
        + half
        + [pl.BlockSpec(memory_space=pl.ANY) for _ in before],
        out_specs=[
            pl.BlockSpec((1, d, hid // 2), lambda e, h: (begin + e, 0, h)),
            pl.BlockSpec((1, hid // 2, d), lambda e, h: (begin + e, h, 0)),
        ],
        out_shape=[
            jax.ShapeDtypeStruct((local, d, hid), BF16),
            jax.ShapeDtypeStruct((local, hid, d), BF16),
        ],
        input_output_aliases={4 * n + k: k for k in range(len(before))},
        **params(4 * n * rows * d * hid * count, "weight_grads"),
    )(*shared, *acts, *ogs, *pgs, *before)


def rows_kernel(tasks, cols, bases, sizes, ids_ref, *refs):
    n = len(bases)
    parts, pairs = refs[:n], refs[n : 2 * n]
    feat_ref, tile_ref, shared_ref = refs[2 * n : 2 * n + 3]
    cross_ref, bias_ref, gating_ref, offset_ref, every_ref, pair_ref = refs[2 * n + 3 :]
    for k, (base, (half, slot)) in enumerate(zip(bases, sizes)):
        shares, blocks, quarter, _ = parts[k].shape
        block = quarter * tasks
        for s in range(shares):
            place = ids_ref[1 + (2 - half) * tasks + slot + s] * quarter
            for j in range(blocks):
                rows = pl.ds(pl.multiple_of(base + j * block + place, quarter), quarter)
                every_ref[rows, :] = parts[k][s, j]
                pair_ref[rows, :] = pairs[k][s, j]
    scaled = (every_ref[...].astype(F32) * tile_ref[...].astype(F32)).astype(BF16)
    cross_ref[...] = mm(feat_ref[...], scaled, TN)
    bias_ref[...] = jnp.sum(scaled.astype(F32), axis=0, keepdims=True)
    pair = pair_ref[...]
    gating_ref[...] = mm(pair[:, :cols], shared_ref[...], TN)
    offset = jnp.sum(pair.astype(F32), axis=0, keepdims=True)
    offset_ref[...] = offset[:, :cols] + offset[:, cols:]


def rows_grads(ids, found, feat, shared, cols, tasks):
    rows, d = feat.shape
    tile = 512
    parts, bases, sizes = [], [], []
    for half, (base, some) in enumerate(found):
        slot = 0
        for part in some:
            parts.append(part)
            bases.append(base)
            sizes.append((half % 2, slot))
            slot += part.shape[0]
    wide = parts[0].shape[-1] - d
    column = lambda j: (0, j)
    return pl.pallas_call(
        functools.partial(rows_kernel, tasks, cols, bases, sizes),
        grid=(d // tile,),
        in_specs=[pl.BlockSpec(memory_space=pltpu.SMEM)]
        + [pl.BlockSpec(p.shape[:3] + (tile,), lambda j: (0, 0, 0, j)) for p in parts]
        + [pl.BlockSpec(p.shape[:3] + (wide,), lambda j: (0, 0, 0, d // wide)) for p in parts]
        + [
            pl.BlockSpec((rows, d), lambda j: (0, 0), pipeline_mode=pl.Buffered(1)),
            pl.BlockSpec((rows, tile), column),
            pl.BlockSpec((rows, tile), column),
        ],
        out_specs=[
            pl.BlockSpec((d, tile), column),
            pl.BlockSpec((1, tile), column),
            pl.BlockSpec((cols, tile), column),
            pl.BlockSpec((1, cols), lambda j: (0, 0)),
        ],
        out_shape=[
            jax.ShapeDtypeStruct((d, d), F32),
            jax.ShapeDtypeStruct((1, d), F32),
            jax.ShapeDtypeStruct((cols, d), F32),
            jax.ShapeDtypeStruct((1, cols), F32),
        ],
        scratch_shapes=[pltpu.VMEM((rows, tile), BF16), pltpu.VMEM((rows, wide), BF16)],
        **params(2 * rows * d * d, "rows_grads"),
    )(ids, *parts, *parts, feat, feat, shared)


def added(parts):
    return sum(p.astype(F32) for p in parts)


class Ring:
    def __init__(self, dp, expert):
        size = dp * expert

        def pairs(move):
            found = []
            for i in range(size):
                z, c, q = i // expert // 2, i // expert % 2, i % expert
                z, c, q = move(z, c, q)
                found.append((i, (z * 2 + c) * expert + q))
            return found

        self.core_pairs = pairs(lambda z, c, q: (z, 1 - c, q))
        self.z1_pairs = pairs(lambda z, c, q: (z ^ 1, c, q))
        self.z3_pairs = pairs(lambda z, c, q: (z ^ 3, c, q))
        self.e1_pairs = pairs(lambda z, c, q: (z, c, q ^ (1, 2)[c]))
        self.e2_pairs = pairs(lambda z, c, q: (z, c, q ^ (2, 1)[c]))

        places = [tuple((0, t) for t in range(4))]
        for k, j in ((1, 0), (4, 0), (4, 1)):
            places.append(((k, 0, j), (k + 1, 0, j), (k + 2, 0, j), (k + 2, 1, j)))
        self.places, self.blocks = tuple(places), 8

    def move(self, x, pairs):
        return lax.ppermute(x, ("dp", "expert"), pairs)

    def core(self, x):
        return self.move(x, self.core_pairs)

    def orders(self):
        q, c = lax.axis_index("expert"), lax.axis_index("dp") % 2
        b1, b2 = 1 + c, 2 - c
        return [q, q ^ b2, q ^ b1, q ^ 3], [q, q ^ b1, q ^ b2, q ^ 3]

    def ids(self, first, tasks):
        mine, other = self.orders()
        plain = list(range(tasks))
        ids = [first]
        for order in (mine, other):
            for k in range(4):
                ids += plain if k == 0 else (other if order is mine else mine)
                ids += order
        return [jnp.stack([jnp.asarray(i, jnp.int32) for i in ids])]

    def spread(self, x):
        one = self.move(x, self.e1_pairs)
        rest = self.move(jnp.stack([x, one]), self.e2_pairs)
        return x[None], one[None], rest

    def in_order(self, parts, order):
        parts = jnp.concatenate(parts, axis=0)
        place = lambda share: sum(jnp.where(order[i] == share, i, 0) for i in range(4))
        return [lax.dynamic_index_in_dim(parts, place(i), 0, False) for i in range(4)]

    def rows(self, x):
        three, one = self.move(x, self.z3_pairs), self.move(x, self.z1_pairs)
        three, one = lax.optimization_barrier((three, one))
        mine = [x, three, one]
        last = self.move(three, self.z1_pairs)
        both = lambda parts: parts + [self.core(p) for p in parts]
        return [[both(mine), lambda *after: both([tie(last, *after)])]], one, last

    def grads(self, task_grad):
        own = jnp.transpose(task_grad, (1, 0, 2))
        share = lax.dynamic_index_in_dim(task_grad, lax.axis_index("expert"), 1, False)
        core, move = self.core, self.move
        share, own = yield (share, own)
        three, own2 = yield (move(share, self.z3_pairs), core(own))
        a0 = three[None]
        both, a0 = yield (jnp.stack([share, three]), a0)
        b0, a1 = yield (move(both, self.z1_pairs), move(a0, self.e1_pairs))
        b0, out = yield (b0, jnp.stack([a0, a1]))
        b1, a2 = yield (move(b0, self.e1_pairs), move(out, self.e2_pairs))
        out, *a = yield (jnp.stack([b0, b1]), a0, a1, a2)
        b2, *other_a = yield (move(out, self.e2_pairs), *map(core, a))
        lift = lambda x, y, z: [x[None], y[None], z]
        self.near = [[own, *lift(*a), *lift(b0, b1, b2)]]
        b = yield (b0, b1, b2)
        other_b = yield tuple(map(core, b))
        far = [own2, *lift(*other_a), *lift(*other_b)]
        return self.near, [far], self.places

    def reduce(self, parts, scatter):
        ((keep, send),) = parts
        (out,) = yield (send,)
        (got,) = yield (self.core(out),)
        parts = [keep, got]
        (out,) = yield (added([p[2:] for p in parts]).astype(BF16),)
        (got,) = yield (self.move(out, self.e1_pairs),)
        parts = [p[:2] for p in parts] + [got]
        (out,) = yield (added([p[1] for p in parts]).astype(BF16),)
        (got,) = yield (self.move(out, self.e2_pairs),)
        parts = [p[0] for p in parts] + [got]
        half = got.shape[0] // 2
        if scatter:
            (out,) = yield (added([p[half:] for p in parts]).astype(BF16),)
            (got,) = yield (self.move(out, self.z1_pairs),)
            parts = [p[:half] for p in parts] + [got]
            half = half // 2
            (out,) = yield (added([p[half:] for p in parts]).astype(BF16),)
            (got,) = yield (self.move(out, self.z3_pairs),)
            return added([p[:half] for p in parts] + [got])
        shape = (4, -1, got.shape[-1])
        (out,) = yield (added(parts).astype(BF16).reshape(shape),)
        (got,) = yield (self.move(out, self.z1_pairs),)
        out = added([out, jnp.concatenate([got[2:], got[:2]], axis=0)])
        (out,) = yield (out.astype(BF16),)
        (got,) = yield (self.move(out, self.z3_pairs),)
        return added([out, jnp.stack([got[1], got[0], got[3], got[2]])])

    def share_tasks(self, x):
        return self.in_order(self.spread(x), self.orders()[1])

    def share_rows(self, x):
        mine = self.spread(x)
        own = jnp.concatenate(self.in_order([m[:, 0] for m in mine], self.orders()[1]), axis=0)
        other = [self.core(p) for p in mine]
        block = x.shape[1] * 4
        return [(0, mine), (4 * block, other)], own


class Steps:
    def __init__(self, steps):
        self.steps, self.moved, self.value = steps, None, None
        self.operand = self._next(None)

    def _next(self, sent):
        try:
            return self.steps.send(sent)
        except StopIteration as stop:
            self.value = stop.value

    def start(self, *after):
        if self.operand is not None:
            self.moved, self.operand = self._next(tie(self.operand, *after)), None

    def finish(self, *after):
        if self.moved is not None:
            moved, self.moved = self.moved, None
            self.operand = self._next(tie(moved, *after))

    def result(self):
        while self.moved is not None or self.operand is not None:
            self.start()
            self.finish()
        return self.value


def finish(steps, *after):
    moved = tie([s.moved or () for s in steps], *after)
    for one, arrays in zip(steps, moved):
        if one.moved is not None:
            one.moved = arrays
            one.finish()


def tie(x, *others):
    others = [o for o in others if o is not None]
    return lax.optimization_barrier((x, *others))[0] if others else x


class Plain:
    def __init__(self, dp, expert):
        self.dp = dp
        self.count = dp // 8 if dp % 8 == 0 else 1
        self.blocks = dp // self.count

    def ids(self, first, tasks):
        plain = list(range(tasks)) * 2 * self.blocks
        return [jnp.stack([jnp.asarray(i, jnp.int32) for i in (first, *plain)])] * self.count

    def rows(self, x):
        every = lax.all_gather(x, "dp", axis=0, tiled=True)
        blocks = jnp.split(every, self.dp)
        n = self.blocks
        return [[blocks[i : i + n]] for i in range(0, self.dp, n)], None, None

    def grads(self, task_grad):
        every = lax.all_gather(jnp.transpose(task_grad, (1, 0, 2)), "dp", axis=0)
        tasks, half = task_grad.shape[1], self.blocks // 2
        self.places = tuple(tuple((0, i, t) for t in range(tasks)) for i in range(half))
        parts = jnp.split(every, 2 * self.count)
        self.near = [[p] for p in parts[::2]]
        return self.near, [[p] for p in parts[1::2]], self.places
        yield

    def reduce(self, parts, scatter):
        blocks = []
        for part in (p for pair in parts for p in pair):
            part = part.reshape(part.shape[0], self.blocks // 2, -1, part.shape[-1])
            blocks.append(jnp.swapaxes(part.astype(F32), 0, 1))
        blocks = jnp.concatenate(blocks, axis=0)
        own = lax.psum_scatter(blocks, "dp", scatter_dimension=0, tiled=True)[0]
        return lax.psum(own, "expert")
        yield

    def share_tasks(self, x):
        return list(x)

    def share_rows(self, x):
        every = jnp.swapaxes(lax.all_gather(x, "dp", axis=0), 0, 1)
        shares, _, quarter, d = every.shape
        found = []
        for k, part in enumerate(jnp.split(every, 2 * self.count, axis=1)):
            found.append((k * self.blocks // 2 * quarter * shares, [part]))
        return found, x.reshape(-1, d)


def local_step(
    net, features, cross_weight, cross_bias, gate_weight, gate_offset, up_weight, down_weight,
    task_grad,
):
    block, d = features.shape
    tasks = task_grad.shape[1]
    cols = gate_weight.shape[1]
    local = up_weight.shape[0]
    first = lax.axis_index("expert") * local
    ids = net.ids(first, tasks)

    feats, early, late = net.rows(features)
    grads = Steps(net.grads(task_grad))
    grads.start(early)

    lowered = []
    for pieces in feats:
        found, begin = (), 0
        for piece in pieces:
            piece = piece(*found) if callable(piece) else piece
            found = cross(
                piece, cross_weight[0], cross_bias, gate_weight.T, gate_offset[None],
                net.blocks // 2, begin, found, tasks,
            )
            begin += len(piece) // 2
        lowered.append(found)
    feats, shared, gates = zip(*lowered)
    grads.finish(*shared)
    ready = grads.operand
    grads.start()
    done = [() for _ in shared]
    quarter = local // 4
    sizes = (local - 2 * quarter, quarter, quarter) if quarter else (local,)
    begins = list(itertools.accumulate((0, *sizes)))
    for b, size in zip(begins, sizes):
        if b:
            grads.finish(*[found[0] for found in done])
            ready = grads.operand
            grads.start()
        done = [
            forward(tie(low, ready), up_weight, down_weight, b, size, found)
            for low, found in zip(shared, done)
        ]
    acts, slopes, outs = zip(*done)
    grads.finish(*[found[0] for found in done])
    ready = grads.operand
    grads.start()
    n = net.blocks
    mixed = [mix(i, tie(gt, ready), o, n, tasks) for i, gt, o in zip(ids, gates, outs)]
    grads.finish(*[keep for keep, _ in mixed])
    near, places = net.near, net.places
    ready = grads.operand
    grads.start()
    mixed = Steps(net.reduce(mixed, True))
    mixed.start()
    spread = [
        spread_grads(i, g, places, tie(gt, ready), o, 0, (), tasks)
        for i, g, gt, o in zip(ids, near, gates, outs)
    ]
    finish([grads, mixed], *[og for og, _ in spread])
    far = grads.result()[1]
    spread = [
        spread_grads(i, g, places, gt, o, 1, tie(x, mixed.operand), tasks)
        for i, g, gt, o, x in zip(ids, far, gates, outs, spread)
    ]
    back = [None for _ in spread]
    parts = BACKWARD_PARTS if local % BACKWARD_PARTS == 0 else 1
    for k in range(parts):
        ready = mixed.operand
        mixed.start()
        back = [
            backward(
                i, tie(og, ready), slope, up_weight, down_weight, gt, inner, n,
                k * local // parts, local // parts, before, k == parts - 1, tasks,
            )
            for i, (og, inner), slope, gt, before in zip(ids, spread, slopes, gates, back)
        ]
        if k < parts - 1:
            mixed.finish(*[x[0] for x in back])
    ogs = [og for og, _ in spread]
    pgs = [b[0] for b in back]
    total = Steps(net.reduce(tie([b[1:] for b in back], mixed.moved), False))
    total.start()
    total.finish()
    mixed.finish(*pgs)
    weights = ()
    for b, size in zip(begins, sizes):
        ready = (mixed.operand, total.operand)
        total.start()
        mixed.start()
        tied = [tie(a, *ready) for a in acts]
        weights = weight_grads(shared, tied, ogs, pgs, b, size, weights)
        finish([total, mixed], weights[0])
    up_grad, down_grad = weights
    total = total.result()
    task_mixed = mixed.result().astype(BF16)
    task_mixed = jnp.stack(net.share_tasks(task_mixed), axis=1)

    logit = total[..., d : d + cols] + total[..., d + cols :]
    high = logit.astype(BF16)
    low = (logit - high.astype(F32)).astype(BF16)
    upstream = total[..., :d] + lax.dot_general(
        high, gate_weight, (((high.ndim - 1,), (1,)), ((), ())), preferred_element_type=F32
    )
    every, own = net.share_rows(jnp.concatenate([upstream.astype(BF16), high, low], axis=-1))
    feats, shared = (x[0] if len(x) == 1 else jnp.concatenate(x, axis=0) for x in (feats, shared))
    cross_grad, bias_grad, gating_grad, offset_grad = rows_grads(
        ids[0], every, feats, shared, cols, tasks
    )

    update = mm(features, cross_weight[0]) + cross_bias
    upstream = own[:, :d].astype(F32)
    scaled = (upstream * features.astype(F32)).astype(BF16)
    feature_grad = (upstream + mm(scaled, cross_weight[0], NT) + upstream * update).astype(BF16)
    return (
        task_mixed,
        feature_grad,
        up_grad,
        down_grad,
        cross_grad[None],
        bias_grad,
        gating_grad.T,
        offset_grad[0],
    )


def solution(mesh):
    dp, expert = mesh.shape["dp"], mesh.shape["expert"]
    net = (Ring if (dp, expert) == (8, 4) else Plain)(dp, expert)
    return jax.shard_map(
        functools.partial(local_step, net),
        mesh=mesh,
        in_specs=(
            P("dp", None),
            P(),
            P(),
            P(),
            P(),
            P("expert", None, "dp"),
            P("expert", "dp", None),
            P("dp", None, None),
        ),
        out_specs=(
            P("dp", None, None),
            P("dp", None),
            P("expert", None, "dp"),
            P("expert", "dp", None),
            P(),
            P(),
            P(),
            P(),
        ),
        check_vma=False,
    )
```

```python
import functools
import itertools

import jax
import jax.numpy as jnp
from jax import lax
from jax.experimental import pallas as pl
from jax.experimental.pallas import tpu as pltpu
from jax.sharding import PartitionSpec as P

F32 = jnp.float32
BF16 = jnp.bfloat16
NN = (((1,), (0,)), ((), ()))
NT = (((1,), (1,)), ((), ()))
TN = (((0,), (0,)), ((), ()))
VMEM_LIMIT = 56 * 2**20
BACKWARD_PARTS = 1


def mm(a, b, dims=NN):
    return lax.dot_general(a, b, dims, preferred_element_type=F32)


def exact(values, ones):
    high = values.astype(BF16)
    low = (values - high.astype(F32)).astype(BF16)
    return mm(high, ones) + mm(low, ones)


def shift(values, size):
    assert size & (size - 1) == 0
    return lax.shift_right_logical(values, jnp.int32(size.bit_length() - 1))


def group_sum(values, experts):
    n = values.shape[1]
    row = shift(lax.broadcasted_iota(jnp.int32, (n, n), 0), experts)
    lane = shift(lax.broadcasted_iota(jnp.int32, (n, n), 1), experts)
    return exact(values, jnp.where(row == lane, 1.0, 0.0).astype(BF16))


def params(flops, name):
    return dict(
        compiler_params=pltpu.CompilerParams(vmem_limit_bytes=VMEM_LIMIT),
        cost_estimate=pl.CostEstimate(flops=flops, bytes_accessed=2**24, transcendentals=0),
        name=name,
    )


def cross_kernel(experts, n, *refs):
    feats, (cw_ref, cb_ref, gw_ref, go_ref) = refs[: 2 * n], refs[2 * n : 2 * n + 4]
    every_ref, shared_ref, gates_ref = refs[-3:]
    block = feats[0].shape[0]

    def half(feats):
        base = jnp.concatenate([f[...] for f in feats], axis=0)
        part = pl.ds(0, n * block)
        every_ref[part, :] = base
        wide = base.astype(F32)
        update = mm(base, cw_ref[...]) + cb_ref[...]
        shared = (wide * update + wide).astype(BF16)
        shared_ref[part, :] = shared
        expo = jnp.exp(mm(shared, gw_ref[...], NT) + go_ref[...])
        gates_ref[part, :] = expo / group_sum(expo, experts)

    pl.when(pl.program_id(0) == 0)(lambda: half(feats[:n]))
    pl.when(pl.program_id(0) == 1)(lambda: half(feats[n:]))


def cross(feats, cw, cb, gw, go, blocks, begin, before, tasks):
    block, d = feats[0].shape
    n = len(feats) // 2
    rows = 2 * blocks * block
    cols = gw.shape[0]
    vmem = pl.BlockSpec(memory_space=pltpu.VMEM)
    size = blocks if begin == 0 else n
    place = lambda i: ((i * blocks + begin) // size, 0)
    return pl.pallas_call(
        functools.partial(cross_kernel, cols // tasks, n),
        grid=(2,),
        in_specs=[vmem] * (len(feats) + 4) + [pl.BlockSpec(memory_space=pl.ANY) for _ in before],
        out_specs=[
            pl.BlockSpec((size * block, d), place),
            pl.BlockSpec((size * block, d), place),
            pl.BlockSpec((size * block, cols), place),
        ],
        out_shape=[
            jax.ShapeDtypeStruct((rows, d), BF16),
            jax.ShapeDtypeStruct((rows, d), BF16),
            jax.ShapeDtypeStruct((rows, cols), F32),
        ],
        input_output_aliases={len(feats) + 4 + k: k for k in range(len(before))},
        **params(n * 4 * block * d * d, "cross"),
    )(*feats, cw, cb, gw, go, *before)


def forward_kernel(shared_ref, up_ref, down_ref, *refs):
    act_ref, slope_ref, out_ref = refs[-3:]
    pre = mm(shared_ref[...], up_ref[0])
    sig = jax.nn.sigmoid(pre)
    act = pre * sig
    low = act.astype(BF16)
    act_ref[0] = low
    slope_ref[0] = (sig + act * (1.0 - sig)).astype(BF16)
    out_ref[0] = mm(low, down_ref[0]).astype(BF16)


def forward(shared, up, down, begin, count, before):
    rows, d = shared.shape
    local, _, hid = up.shape
    sub = min(rows, 512)
    here = lambda e, r: (begin + e, r, 0)
    there = lambda e, r: (begin + e, 0, 0)
    wide = jax.ShapeDtypeStruct((local, rows, hid), BF16)
    return pl.pallas_call(
        forward_kernel,
        grid=(count, rows // sub),
        in_specs=[
            pl.BlockSpec((sub, d), lambda e, r: (r, 0)),
            pl.BlockSpec((1, d, hid), there),
            pl.BlockSpec((1, hid, d), there),
        ]
        + [pl.BlockSpec(memory_space=pl.ANY) for _ in before],
        out_specs=[
            pl.BlockSpec((1, sub, hid), here),
            pl.BlockSpec((1, sub, hid), here),
            pl.BlockSpec((1, sub, d), here),
        ],
        out_shape=[wide, wide, jax.ShapeDtypeStruct((local, rows, d), BF16)],
        input_output_aliases={3 + k: k for k in range(len(before))},
        **params(4 * rows * d * hid * count, "forward"),
    )(shared, up, down, *before)


def same_row(n, m, group):
    row = lax.broadcasted_iota(jnp.int32, (n, m), 0) & (group - 1)
    lane = lax.broadcasted_iota(jnp.int32, (1, m), 1) & (group - 1)
    return jnp.where(row == lane, 1.0, 0.0)


def chosen(ids_ref, order, by_task, tasks, local, experts, cols, group):
    wide = tasks * local * group
    lane = shift(lax.broadcasted_iota(jnp.int32, (1, wide), 1), group)
    task = shift(lane, local) if by_task else lane & (tasks - 1)
    expert = lane & (local - 1) if by_task else shift(lane, tasks)
    ids = jnp.zeros_like(lane) + ids_ref[order]
    for t in range(1, tasks):
        ids = jnp.where(task == t, ids_ref[order + t], ids)
    row = lax.broadcasted_iota(jnp.int32, (cols, wide), 0)
    return jnp.where(row == ids * experts + ids_ref[0] + expert, 1.0, 0.0).astype(BF16)


def stack(weights, r, group, count, width):
    return jnp.concatenate(
        [weights[r : r + group, j * width : (j + 1) * width] for j in range(count)], axis=0
    )


def mix_kernel(tasks, experts, block, ids_ref, gates_ref, outs_ref, keep_ref, send_ref):
    i = pl.program_id(0)
    rows, cols = gates_ref.shape
    local = outs_ref.shape[0]
    group = 256 // local
    flat = same_row(block, tasks * local * group, group)
    step = rows // block

    def write(ref):
        for k in range(step):
            at = pl.ds(k * block, block)
            order = 1 + 2 * tasks * (i * step + k) + tasks
            weights = mm(
                gates_ref[at, :].astype(BF16),
                chosen(ids_ref, order, True, tasks, local, experts, cols, group),
            )
            weights = (weights * flat).astype(BF16)
            for r in range(0, block, group):
                part = pl.ds(k * block + r, group)
                out = jnp.concatenate([outs_ref[j, part, :] for j in range(local)], axis=0)
                both = mm(stack(weights, r, group, tasks, local * group), out).astype(BF16)
                for t in range(tasks):
                    ref[t, part, :] = both[t * group : (t + 1) * group]

    pl.when(i < pl.num_programs(0) // 2)(lambda: write(keep_ref))
    pl.when(i >= pl.num_programs(0) // 2)(lambda: write(send_ref))


def mix(ids, gates, outs, n, tasks):
    local, rows, d = outs.shape
    cols = gates.shape[1]
    sub = rows // 4
    return pl.pallas_call(
        functools.partial(mix_kernel, tasks, cols // tasks, rows // n),
        grid_spec=pltpu.PrefetchScalarGridSpec(
            num_scalar_prefetch=1,
            grid=(4,),
            in_specs=[
                pl.BlockSpec((sub, cols), lambda i, f: (i, 0)),
                pl.BlockSpec((local, sub, d), lambda i, f: (0, i, 0)),
            ],
            out_specs=[
                pl.BlockSpec((tasks, sub, d), lambda i, f: (0, jnp.minimum(i, 1), 0)),
                pl.BlockSpec((tasks, sub, d), lambda i, f: (0, jnp.maximum(i - 2, 0), 0)),
            ],
        ),
        out_shape=[jax.ShapeDtypeStruct((tasks, rows // 2, d), BF16)] * 2,
        **params(2**11 * rows * d, "mix"),
    )(ids, gates, outs)


def spread_kernel(tasks, experts, places, n_grads, begin, ids_ref, *refs):
    grads = refs[:n_grads]
    gates_ref, outs_ref = refs[n_grads : n_grads + 2]
    og_ref, inner_ref, rows_ref, sems = refs[-4:]
    i = pl.program_id(0)
    rows, cols = gates_ref.shape
    count = rows_ref.shape[1]
    block = rows // count
    local = og_ref.shape[0]
    group = 256 // local

    def fetch(step, slot, act):
        for k in range(len(places) // count):

            @pl.when(step == k)
            def _():
                for j in range(count):
                    for t, (which, *lead) in enumerate(places[k * count + j]):
                        act(
                            pltpu.make_async_copy(
                                grads[which].at[tuple(lead)],
                                rows_ref.at[slot, j, t],
                                sems.at[slot, j, t],
                            )
                        )

    @pl.when(i == 0)
    def _():
        fetch(0, 0, lambda copy: copy.start())

    fetch(i + 1, (i + 1) & 1, lambda copy: copy.start())
    flat = same_row(block, tasks * local * group, group)
    square = same_row(tasks * group, local * group, group)
    fetch(i, i & 1, lambda copy: copy.wait())
    slot = i & 1
    for k in range(count):
        order = 1 + 2 * tasks * ((begin + i) * count + k)
        at = pl.ds(k * block, block)
        gates = gates_ref[at, :]
        pick = lambda by_task: chosen(
            ids_ref, order, by_task, tasks, local, experts, cols, group
        )
        weights = (mm(gates.astype(BF16), pick(False)) * flat).astype(BF16)
        inners = []
        for r in range(0, block, group):
            part = pl.ds(k * block + r, group)
            grad = jnp.concatenate(
                [rows_ref[slot, k, t, r : r + group, :] for t in range(tasks)], axis=0
            )
            out = jnp.concatenate([outs_ref[j, part, :] for j in range(local)], axis=0)
            both = mm(stack(weights, r, group, local, tasks * group), grad).astype(BF16)
            for j in range(local):
                og_ref[j, part, :] = both[j * group : (j + 1) * group]
            products = mm(grad, out, NT) * square
            inners.append(
                jnp.concatenate(
                    [products[t * group : (t + 1) * group] for t in range(tasks)], axis=1
                )
            )
        inner = jnp.concatenate(inners, axis=0)
        high = inner.astype(BF16)
        rest = (inner - high.astype(F32)).astype(BF16)
        at_column = pick(True)
        inner_ref[at, :] = mm(high, at_column, NT) + mm(rest, at_column, NT)


def spread_grads(ids, grads, places, gates, outs, begin, before, tasks):
    local, rows, d = outs.shape
    cols = gates.shape[1]
    n = len(places)
    count = 1
    block = rows // 2 // n
    sub = count * block
    begin = begin * (n // count)
    every = lambda i, f: (0, begin + i, 0)
    here = lambda i, f: (begin + i, 0)
    return pl.pallas_call(
        functools.partial(spread_kernel, tasks, cols // tasks, places, len(grads), begin),
        grid_spec=pltpu.PrefetchScalarGridSpec(
            num_scalar_prefetch=1,
            grid=(n // count,),
            in_specs=[pl.BlockSpec(memory_space=pl.ANY) for _ in grads]
            + [pl.BlockSpec((sub, cols), here), pl.BlockSpec((local, sub, d), every)]
            + [pl.BlockSpec(memory_space=pl.ANY) for _ in before],
            out_specs=[
                pl.BlockSpec((local, sub, d), every),
                pl.BlockSpec((sub, cols), here),
            ],
            scratch_shapes=[
                pltpu.VMEM((2, count, tasks, block, d), BF16),
                pltpu.SemaphoreType.DMA((2, count, tasks)),
            ],
        ),
        out_shape=[
            jax.ShapeDtypeStruct((local, rows, d), BF16),
            jax.ShapeDtypeStruct((rows, cols), F32),
        ],
        input_output_aliases={3 + len(grads) + k: k for k in range(len(before))},
        **params(2**10 * rows * d, "spread_grads"),
    )(ids, *grads, gates, outs, *before)


def backward_kernel(tasks, experts, n, sub, start, last, ids_ref, *refs):
    og_ref, slope_ref, up_ref, down_ref = refs[:4]
    total_ref = None if start else refs[4]
    if last:
        gates_ref, inner_ref = refs[5 - start : 7 - start]
        pg_ref, keep_ref, send_ref, acc_ref, pair_ref = refs[-5:]
    else:
        pg_ref, acc_ref = refs[-2:]
    e = pl.program_id(0)
    rows, d = acc_ref.shape

    for r in range(0, rows, sub):
        part = pl.ds(r, sub)
        hidden = mm(og_ref[0, part, :], down_ref[0], NT)
        pre_grad = (hidden * slope_ref[0, part, :].astype(F32)).astype(BF16)
        pg_ref[0, part, :] = pre_grad
        found = mm(pre_grad, up_ref[0], NT)

        @pl.when(e == 0)
        def _():
            acc_ref[part, :] = found if start else total_ref[part, :] + found

        @pl.when(e > 0)
        def _():
            acc_ref[part, :] += found

    if not last:
        return
    cols = gates_ref.shape[1]
    block = rows // n
    quarter = block // tasks

    @pl.when(e == 0)
    def _():
        gates, inner = gates_ref[...], inner_ref[...]
        logit = gates * (inner - group_sum(gates * inner, experts))
        high = logit.astype(BF16)
        rest = (logit - high.astype(F32)).astype(BF16)
        row = lax.broadcasted_iota(jnp.int32, (cols, 2 * cols), 0)
        lane = lax.broadcasted_iota(jnp.int32, (cols, 2 * cols), 1)
        one = jnp.where(lane == row, 1.0, 0.0).astype(BF16)
        two = jnp.where(lane == row + cols, 1.0, 0.0).astype(BF16)
        pair_ref[...] = (mm(high, one) + mm(rest, two)).astype(BF16)

    @pl.when(e == pl.num_programs(0) - 1)
    def _():
        for i in range(n):
            ref = keep_ref if i < n // 2 else send_ref
            for t in range(tasks):
                place = ids_ref[1 + 2 * tasks * i + tasks + t]
                begin = pl.multiple_of(i * block + place * quarter, quarter)
                source = pl.ds(begin, quarter)
                dest = pl.ds(i % (n // 2) * quarter, quarter)
                ref[t, dest, :d] = acc_ref[source, :].astype(BF16)
                ref[t, dest, d:] = pair_ref[source, :]


def backward(ids, og, slope, up, down, gates, inner, n, begin, count, before, last, tasks):
    local, rows, d = og.shape
    hid = up.shape[2]
    here = lambda e, f: (begin + e, 0, 0)
    cols = gates.shape[1]
    width = d + 2 * cols
    packed = (tasks, rows // 2 // tasks, width)
    start = before is None
    whole = lambda shape, **how: pl.BlockSpec(shape, lambda e, f: (0,) * len(shape), **how)
    specs, shapes, scratch = [whole((rows, d))], [jax.ShapeDtypeStruct((rows, d), F32)], []
    if last:
        specs, shapes = [whole(packed)] * 2, [jax.ShapeDtypeStruct(packed, BF16)] * 2
        scratch = [pltpu.VMEM((rows, d), F32), pltpu.VMEM((rows, 2 * cols), BF16)]
    args, in_specs = [], []
    if not start:
        args, in_specs = [before[1]], [whole((rows, d), pipeline_mode=pl.Buffered(1))]
    if last:
        args, in_specs = args + [gates, inner], in_specs + [whole((rows, cols))] * 2
    if not start:
        args, in_specs = args + [before[0]], in_specs + [pl.BlockSpec(memory_space=pl.ANY)]
    return pl.pallas_call(
        functools.partial(
            backward_kernel, tasks, cols // tasks, n, min(rows, 512), start, last
        ),
        grid_spec=pltpu.PrefetchScalarGridSpec(
            num_scalar_prefetch=1,
            grid=(count,),
            in_specs=[
                pl.BlockSpec((1, rows, d), here),
                pl.BlockSpec((1, rows, hid), here),
                pl.BlockSpec((1, d, hid), here),
                pl.BlockSpec((1, hid, d), here),
            ]
            + in_specs,
            out_specs=[pl.BlockSpec((1, rows, hid), here)] + specs,
            scratch_shapes=scratch,
        ),
        out_shape=[jax.ShapeDtypeStruct((local, rows, hid), BF16)] + shapes,
        input_output_aliases={} if start else {4 + len(args): 0},
        **params(4 * rows * d * hid * count, "backward"),
    )(ids, og, slope, up, down, *args)


def weights_kernel(n, *refs):
    shared, acts, ogs, pgs = (refs[k * n : (k + 1) * n] for k in range(4))
    up_ref, down_ref = refs[-2:]
    total = sum(mm(s[...], p[0], TN) for s, p in zip(shared, pgs))
    up_ref[0] = total.astype(BF16)
    total = sum(mm(a[0], o[0], TN) for a, o in zip(acts, ogs))
    down_ref[0] = total.astype(BF16)


def weight_grads(shared, acts, ogs, pgs, begin, count, before):
    local, rows, hid = acts[0].shape
    d = shared[0].shape[1]
    n = len(shared)
    there = lambda e, h: (begin + e, 0, 0)
    half = [pl.BlockSpec((1, x.shape[1], hid // 2), lambda e, h: (begin + e, 0, h)) for x in acts]
    return pl.pallas_call(
        functools.partial(weights_kernel, n),
        grid=(count, 2),
        in_specs=[pl.BlockSpec(s.shape, lambda e, h: (0, 0)) for s in shared]
        + half
        + [pl.BlockSpec((1,) + x.shape[1:], there) for x in ogs]
        + half
        + [pl.BlockSpec(memory_space=pl.ANY) for _ in before],
        out_specs=[
            pl.BlockSpec((1, d, hid // 2), lambda e, h: (begin + e, 0, h)),
            pl.BlockSpec((1, hid // 2, d), lambda e, h: (begin + e, h, 0)),
        ],
        out_shape=[
            jax.ShapeDtypeStruct((local, d, hid), BF16),
            jax.ShapeDtypeStruct((local, hid, d), BF16),
        ],
        input_output_aliases={4 * n + k: k for k in range(len(before))},
        **params(4 * n * rows * d * hid * count, "weight_grads"),
    )(*shared, *acts, *ogs, *pgs, *before)


def rows_kernel(tasks, cols, bases, sizes, ids_ref, *refs):
    n = len(bases)
    parts, pairs = refs[:n], refs[n : 2 * n]
    feat_ref, tile_ref, shared_ref = refs[2 * n : 2 * n + 3]
    cross_ref, bias_ref, gating_ref, offset_ref, every_ref, pair_ref = refs[2 * n + 3 :]
    for k, (base, (half, slot)) in enumerate(zip(bases, sizes)):
        shares, blocks, quarter, _ = parts[k].shape
        block = quarter * tasks
        for s in range(shares):
            place = ids_ref[1 + (2 - half) * tasks + slot + s] * quarter
            for j in range(blocks):
                rows = pl.ds(pl.multiple_of(base + j * block + place, quarter), quarter)
                every_ref[rows, :] = parts[k][s, j]
                pair_ref[rows, :] = pairs[k][s, j]
    scaled = (every_ref[...].astype(F32) * tile_ref[...].astype(F32)).astype(BF16)
    cross_ref[...] = mm(feat_ref[...], scaled, TN)
    bias_ref[...] = jnp.sum(scaled.astype(F32), axis=0, keepdims=True)
    pair = pair_ref[...]
    gating_ref[...] = mm(pair[:, :cols], shared_ref[...], TN)
    offset = jnp.sum(pair.astype(F32), axis=0, keepdims=True)
    offset_ref[...] = offset[:, :cols] + offset[:, cols:]


def rows_grads(ids, found, feat, shared, cols, tasks):
    rows, d = feat.shape
    tile = 512
    parts, bases, sizes = [], [], []
    for half, (base, some) in enumerate(found):
        slot = 0
        for part in some:
            parts.append(part)
            bases.append(base)
            sizes.append((half % 2, slot))
            slot += part.shape[0]
    wide = parts[0].shape[-1] - d
    column = lambda j: (0, j)
    return pl.pallas_call(
        functools.partial(rows_kernel, tasks, cols, bases, sizes),
        grid=(d // tile,),
        in_specs=[pl.BlockSpec(memory_space=pltpu.SMEM)]
        + [pl.BlockSpec(p.shape[:3] + (tile,), lambda j: (0, 0, 0, j)) for p in parts]
        + [pl.BlockSpec(p.shape[:3] + (wide,), lambda j: (0, 0, 0, d // wide)) for p in parts]
        + [
            pl.BlockSpec((rows, d), lambda j: (0, 0), pipeline_mode=pl.Buffered(1)),
            pl.BlockSpec((rows, tile), column),
            pl.BlockSpec((rows, tile), column),
        ],
        out_specs=[
            pl.BlockSpec((d, tile), column),
            pl.BlockSpec((1, tile), column),
            pl.BlockSpec((cols, tile), column),
            pl.BlockSpec((1, cols), lambda j: (0, 0)),
        ],
        out_shape=[
            jax.ShapeDtypeStruct((d, d), F32),
            jax.ShapeDtypeStruct((1, d), F32),
            jax.ShapeDtypeStruct((cols, d), F32),
            jax.ShapeDtypeStruct((1, cols), F32),
        ],
        scratch_shapes=[pltpu.VMEM((rows, tile), BF16), pltpu.VMEM((rows, wide), BF16)],
        **params(2 * rows * d * d, "rows_grads"),
    )(ids, *parts, *parts, feat, feat, shared)


def added(parts):
    return sum(p.astype(F32) for p in parts)


class Ring:
    def __init__(self, dp, expert):
        size = dp * expert

        def pairs(move):
            found = []
            for i in range(size):
                z, c, q = i // expert // 2, i // expert % 2, i % expert
                z, c, q = move(z, c, q)
                found.append((i, (z * 2 + c) * expert + q))
            return found

        self.core_pairs = pairs(lambda z, c, q: (z, 1 - c, q))
        self.z1_pairs = pairs(lambda z, c, q: (z ^ 1, c, q))
        self.z3_pairs = pairs(lambda z, c, q: (z ^ 3, c, q))
        self.e1_pairs = pairs(lambda z, c, q: (z, c, q ^ (1, 2)[c]))
        self.e2_pairs = pairs(lambda z, c, q: (z, c, q ^ (2, 1)[c]))

        places = [tuple((0, t) for t in range(4))]
        for k, j in ((1, 0), (4, 0), (4, 1)):
            places.append(((k, 0, j), (k + 1, 0, j), (k + 2, 0, j), (k + 2, 1, j)))
        self.places, self.blocks = tuple(places), 8

    def move(self, x, pairs):
        return lax.ppermute(x, ("dp", "expert"), pairs)

    def core(self, x):
        return self.move(x, self.core_pairs)

    def orders(self):
        q, c = lax.axis_index("expert"), lax.axis_index("dp") % 2
        b1, b2 = 1 + c, 2 - c
        return [q, q ^ b2, q ^ b1, q ^ 3], [q, q ^ b1, q ^ b2, q ^ 3]

    def ids(self, first, tasks):
        mine, other = self.orders()
        plain = list(range(tasks))
        ids = [first]
        for order in (mine, other):
            for k in range(4):
                ids += plain if k == 0 else (other if order is mine else mine)
                ids += order
        return [jnp.stack([jnp.asarray(i, jnp.int32) for i in ids])]

    def spread(self, x):
        one = self.move(x, self.e1_pairs)
        rest = self.move(jnp.stack([x, one]), self.e2_pairs)
        return x[None], one[None], rest

    def in_order(self, parts, order):
        parts = jnp.concatenate(parts, axis=0)
        place = lambda share: sum(jnp.where(order[i] == share, i, 0) for i in range(4))
        return [lax.dynamic_index_in_dim(parts, place(i), 0, False) for i in range(4)]

    def rows(self, x):
        three, one = self.move(x, self.z3_pairs), self.move(x, self.z1_pairs)
        three, one = lax.optimization_barrier((three, one))
        mine = [x, three, one]
        last = self.move(three, self.z1_pairs)
        both = lambda parts: parts + [self.core(p) for p in parts]
        return [[both(mine), lambda *after: both([tie(last, *after)])]], one, last

    def grads(self, task_grad):
        own = jnp.transpose(task_grad, (1, 0, 2))
        share = lax.dynamic_index_in_dim(task_grad, lax.axis_index("expert"), 1, False)
        core, move = self.core, self.move
        share, own = yield (share, own)
        three, own2 = yield (move(share, self.z3_pairs), core(own))
        a0 = three[None]
        both, a0 = yield (jnp.stack([share, three]), a0)
        b0, a1 = yield (move(both, self.z1_pairs), move(a0, self.e1_pairs))
        b0, out = yield (b0, jnp.stack([a0, a1]))
        b1, a2 = yield (move(b0, self.e1_pairs), move(out, self.e2_pairs))
        out, *a = yield (jnp.stack([b0, b1]), a0, a1, a2)
        b2, *other_a = yield (move(out, self.e2_pairs), *map(core, a))
        lift = lambda x, y, z: [x[None], y[None], z]
        self.near = [[own, *lift(*a), *lift(b0, b1, b2)]]
        b = yield (b0, b1, b2)
        other_b = yield tuple(map(core, b))
        far = [own2, *lift(*other_a), *lift(*other_b)]
        return self.near, [far], self.places

    def reduce(self, parts, scatter):
        ((keep, send),) = parts
        (out,) = yield (send,)
        (got,) = yield (self.core(out),)
        parts = [keep, got]
        (out,) = yield (added([p[2:] for p in parts]).astype(BF16),)
        (got,) = yield (self.move(out, self.e1_pairs),)
        parts = [p[:2] for p in parts] + [got]
        (out,) = yield (added([p[1] for p in parts]).astype(BF16),)
        (got,) = yield (self.move(out, self.e2_pairs),)
        parts = [p[0] for p in parts] + [got]
        half = got.shape[0] // 2
        if scatter:
            (out,) = yield (added([p[half:] for p in parts]).astype(BF16),)
            (got,) = yield (self.move(out, self.z1_pairs),)
            parts = [p[:half] for p in parts] + [got]
            half = half // 2
            (out,) = yield (added([p[half:] for p in parts]).astype(BF16),)
            (got,) = yield (self.move(out, self.z3_pairs),)
            return added([p[:half] for p in parts] + [got])
        shape = (4, -1, got.shape[-1])
        (out,) = yield (added(parts).astype(BF16).reshape(shape),)
        (got,) = yield (self.move(out, self.z1_pairs),)
        out = added([out, jnp.concatenate([got[2:], got[:2]], axis=0)])
        (out,) = yield (out.astype(BF16),)
        (got,) = yield (self.move(out, self.z3_pairs),)
        return added([out, jnp.stack([got[1], got[0], got[3], got[2]])])

    def share_tasks(self, x):
        return self.in_order(self.spread(x), self.orders()[1])

    def share_rows(self, x):
        mine = self.spread(x)
        own = jnp.concatenate(self.in_order([m[:, 0] for m in mine], self.orders()[1]), axis=0)
        other = [self.core(p) for p in mine]
        block = x.shape[1] * 4
        return [(0, mine), (4 * block, other)], own


class Steps:
    def __init__(self, steps):
        self.steps, self.moved, self.value = steps, None, None
        self.operand = self._next(None)

    def _next(self, sent):
        try:
            return self.steps.send(sent)
        except StopIteration as stop:
            self.value = stop.value

    def start(self, *after):
        if self.operand is not None:
            self.moved, self.operand = self._next(tie(self.operand, *after)), None

    def finish(self, *after):
        if self.moved is not None:
            moved, self.moved = self.moved, None
            self.operand = self._next(tie(moved, *after))

    def result(self):
        while self.moved is not None or self.operand is not None:
            self.start()
            self.finish()
        return self.value


def finish(steps, *after):
    moved = tie([s.moved or () for s in steps], *after)
    for one, arrays in zip(steps, moved):
        if one.moved is not None:
            one.moved = arrays
            one.finish()


def tie(x, *others):
    others = [o for o in others if o is not None]
    return lax.optimization_barrier((x, *others))[0] if others else x


class Plain:
    def __init__(self, dp, expert):
        self.dp = dp
        self.count = dp // 8 if dp % 8 == 0 else 1
        self.blocks = dp // self.count

    def ids(self, first, tasks):
        plain = list(range(tasks)) * 2 * self.blocks
        return [jnp.stack([jnp.asarray(i, jnp.int32) for i in (first, *plain)])] * self.count

    def rows(self, x):
        every = lax.all_gather(x, "dp", axis=0, tiled=True)
        blocks = jnp.split(every, self.dp)
        n = self.blocks
        return [[blocks[i : i + n]] for i in range(0, self.dp, n)], None, None

    def grads(self, task_grad):
        every = lax.all_gather(jnp.transpose(task_grad, (1, 0, 2)), "dp", axis=0)
        tasks, half = task_grad.shape[1], self.blocks // 2
        self.places = tuple(tuple((0, i, t) for t in range(tasks)) for i in range(half))
        parts = jnp.split(every, 2 * self.count)
        self.near = [[p] for p in parts[::2]]
        return self.near, [[p] for p in parts[1::2]], self.places
        yield

    def reduce(self, parts, scatter):
        blocks = []
        for part in (p for pair in parts for p in pair):
            part = part.reshape(part.shape[0], self.blocks // 2, -1, part.shape[-1])
            blocks.append(jnp.swapaxes(part.astype(F32), 0, 1))
        blocks = jnp.concatenate(blocks, axis=0)
        own = lax.psum_scatter(blocks, "dp", scatter_dimension=0, tiled=True)[0]
        return lax.psum(own, "expert")
        yield

    def share_tasks(self, x):
        return list(x)

    def share_rows(self, x):
        every = jnp.swapaxes(lax.all_gather(x, "dp", axis=0), 0, 1)
        shares, _, quarter, d = every.shape
        found = []
        for k, part in enumerate(jnp.split(every, 2 * self.count, axis=1)):
            found.append((k * self.blocks // 2 * quarter * shares, [part]))
        return found, x.reshape(-1, d)


def local_step(
    net, features, cross_weight, cross_bias, gate_weight, gate_offset, up_weight, down_weight,
    task_grad,
):
    block, d = features.shape
    tasks = task_grad.shape[1]
    cols = gate_weight.shape[1]
    local = up_weight.shape[0]
    first = lax.axis_index("expert") * local
    ids = net.ids(first, tasks)

    feats, early, late = net.rows(features)
    grads = Steps(net.grads(task_grad))
    grads.start(early)

    lowered = []
    for pieces in feats:
        found, begin = (), 0
        for piece in pieces:
            piece = piece(*found, grads.moved) if callable(piece) else piece
            found = cross(
                piece, cross_weight[0], cross_bias, gate_weight.T, gate_offset[None],
                net.blocks // 2, begin, found, tasks,
            )
            begin += len(piece) // 2
        lowered.append(found)
    feats, shared, gates = zip(*lowered)
    grads.finish(*shared)
    ready = grads.operand
    grads.start()
    done = [() for _ in shared]
    quarter = local // 4
    sizes = (local - 2 * quarter, quarter, quarter) if quarter else (local,)
    begins = list(itertools.accumulate((0, *sizes)))
    for b, size in zip(begins, sizes):
        if b:
            grads.finish(*[found[0] for found in done])
            ready = grads.operand
            grads.start()
        done = [
            forward(tie(low, ready), up_weight, down_weight, b, size, found)
            for low, found in zip(shared, done)
        ]
    acts, slopes, outs = zip(*done)
    grads.finish(*[found[0] for found in done])
    ready = grads.operand
    grads.start()
    n = net.blocks
    mixed = [mix(i, tie(gt, ready), o, n, tasks) for i, gt, o in zip(ids, gates, outs)]
    grads.finish(*[keep for keep, _ in mixed])
    near, places = net.near, net.places
    ready = grads.operand
    grads.start()
    mixed = Steps(net.reduce(mixed, True))
    mixed.start()
    spread = [
        spread_grads(i, g, places, tie(gt, ready), o, 0, (), tasks)
        for i, g, gt, o in zip(ids, near, gates, outs)
    ]
    finish([grads, mixed], *[og for og, _ in spread])
    far = grads.result()[1]
    spread = [
        spread_grads(i, g, places, gt, o, 1, tie(x, mixed.operand), tasks)
        for i, g, gt, o, x in zip(ids, far, gates, outs, spread)
    ]
    back = [None for _ in spread]
    parts = BACKWARD_PARTS if local % BACKWARD_PARTS == 0 else 1
    for k in range(parts):
        ready = mixed.operand
        mixed.start()
        back = [
            backward(
                i, tie(og, ready), slope, up_weight, down_weight, gt, inner, n,
                k * local // parts, local // parts, before, k == parts - 1, tasks,
            )
            for i, (og, inner), slope, gt, before in zip(ids, spread, slopes, gates, back)
        ]
        if k < parts - 1:
            mixed.finish(*[x[0] for x in back])
    ogs = [og for og, _ in spread]
    pgs = [b[0] for b in back]
    total = Steps(net.reduce(tie([b[1:] for b in back], mixed.moved), False))
    total.start()
    total.finish()
    mixed.finish(*pgs)
    weights = ()
    for b, size in zip(begins, sizes):
        ready = (mixed.operand, total.operand)
        total.start()
        mixed.start()
        tied = [tie(a, *ready) for a in acts]
        weights = weight_grads(shared, tied, ogs, pgs, b, size, weights)
        finish([total, mixed], weights[0])
    up_grad, down_grad = weights
    total = total.result()
    task_mixed = mixed.result().astype(BF16)
    task_mixed = jnp.stack(net.share_tasks(task_mixed), axis=1)

    logit = total[..., d : d + cols] + total[..., d + cols :]
    high = logit.astype(BF16)
    low = (logit - high.astype(F32)).astype(BF16)
    upstream = total[..., :d] + lax.dot_general(
        high, gate_weight, (((high.ndim - 1,), (1,)), ((), ())), preferred_element_type=F32
    )
    every, own = net.share_rows(jnp.concatenate([upstream.astype(BF16), high, low], axis=-1))
    feats, shared = (x[0] if len(x) == 1 else jnp.concatenate(x, axis=0) for x in (feats, shared))
    cross_grad, bias_grad, gating_grad, offset_grad = rows_grads(
        ids[0], every, feats, shared, cols, tasks
    )

    update = mm(features, cross_weight[0]) + cross_bias
    upstream = own[:, :d].astype(F32)
    scaled = (upstream * features.astype(F32)).astype(BF16)
    feature_grad = (upstream + mm(scaled, cross_weight[0], NT) + upstream * update).astype(BF16)
    return (
        task_mixed,
        feature_grad,
        up_grad,
        down_grad,
        cross_grad[None],
        bias_grad,
        gating_grad.T,
        offset_grad[0],
    )


def solution(mesh):
    dp, expert = mesh.shape["dp"], mesh.shape["expert"]
    net = (Ring if (dp, expert) == (8, 4) else Plain)(dp, expert)
    return jax.shard_map(
        functools.partial(local_step, net),
        mesh=mesh,
        in_specs=(
            P("dp", None),
            P(),
            P(),
            P(),
            P(),
            P("expert", None, "dp"),
            P("expert", "dp", None),
            P("dp", None, None),
        ),
        out_specs=(
            P("dp", None, None),
            P("dp", None),
            P("expert", None, "dp"),
            P("expert", "dp", None),
            P(),
            P(),
            P(),
            P(),
        ),
        check_vma=False,
    )
```

```python
import functools
import itertools

import jax
import jax.numpy as jnp
from jax import lax
from jax.experimental import pallas as pl
from jax.experimental.pallas import tpu as pltpu
from jax.sharding import PartitionSpec as P

F32 = jnp.float32
BF16 = jnp.bfloat16
NN = (((1,), (0,)), ((), ()))
NT = (((1,), (1,)), ((), ()))
TN = (((0,), (0,)), ((), ()))
VMEM_LIMIT = 56 * 2**20
BACKWARD_PARTS = 1


def mm(a, b, dims=NN):
    return lax.dot_general(a, b, dims, preferred_element_type=F32)


def exact(values, ones):
    high = values.astype(BF16)
    low = (values - high.astype(F32)).astype(BF16)
    return mm(high, ones) + mm(low, ones)


def shift(values, size):
    assert size & (size - 1) == 0
    return lax.shift_right_logical(values, jnp.int32(size.bit_length() - 1))


def group_sum(values, experts):
    n = values.shape[1]
    row = shift(lax.broadcasted_iota(jnp.int32, (n, n), 0), experts)
    lane = shift(lax.broadcasted_iota(jnp.int32, (n, n), 1), experts)
    return exact(values, jnp.where(row == lane, 1.0, 0.0).astype(BF16))


def params(flops, name):
    return dict(
        compiler_params=pltpu.CompilerParams(vmem_limit_bytes=VMEM_LIMIT),
        cost_estimate=pl.CostEstimate(flops=flops, bytes_accessed=2**24, transcendentals=0),
        name=name,
    )


def cross_kernel(experts, n, *refs):
    feats, (cw_ref, cb_ref, gw_ref, go_ref) = refs[: 2 * n], refs[2 * n : 2 * n + 4]
    every_ref, shared_ref, gates_ref = refs[-3:]
    block = feats[0].shape[0]

    def half(feats):
        base = jnp.concatenate([f[...] for f in feats], axis=0)
        part = pl.ds(0, n * block)
        every_ref[part, :] = base
        wide = base.astype(F32)
        update = mm(base, cw_ref[...]) + cb_ref[...]
        shared = (wide * update + wide).astype(BF16)
        shared_ref[part, :] = shared
        expo = jnp.exp(mm(shared, gw_ref[...], NT) + go_ref[...])
        gates_ref[part, :] = expo / group_sum(expo, experts)

    pl.when(pl.program_id(0) == 0)(lambda: half(feats[:n]))
    pl.when(pl.program_id(0) == 1)(lambda: half(feats[n:]))


def cross(feats, cw, cb, gw, go, blocks, begin, before, tasks):
    block, d = feats[0].shape
    n = len(feats) // 2
    rows = 2 * blocks * block
    cols = gw.shape[0]
    vmem = pl.BlockSpec(memory_space=pltpu.VMEM)
    size = blocks if begin == 0 else n
    place = lambda i: ((i * blocks + begin) // size, 0)
    return pl.pallas_call(
        functools.partial(cross_kernel, cols // tasks, n),
        grid=(2,),
        in_specs=[vmem] * (len(feats) + 4) + [pl.BlockSpec(memory_space=pl.ANY) for _ in before],
        out_specs=[
            pl.BlockSpec((size * block, d), place),
            pl.BlockSpec((size * block, d), place),
            pl.BlockSpec((size * block, cols), place),
        ],
        out_shape=[
            jax.ShapeDtypeStruct((rows, d), BF16),
            jax.ShapeDtypeStruct((rows, d), BF16),
            jax.ShapeDtypeStruct((rows, cols), F32),
        ],
        input_output_aliases={len(feats) + 4 + k: k for k in range(len(before))},
        **params(n * 4 * block * d * d, "cross"),
    )(*feats, cw, cb, gw, go, *before)


def forward_kernel(shared_ref, up_ref, down_ref, *refs):
    act_ref, slope_ref, out_ref = refs[-3:]
    pre = mm(shared_ref[...], up_ref[0])
    sig = jax.nn.sigmoid(pre)
    act = pre * sig
    low = act.astype(BF16)
    act_ref[0] = low
    slope_ref[0] = (sig + act * (1.0 - sig)).astype(BF16)
    out_ref[0] = mm(low, down_ref[0]).astype(BF16)


def forward(shared, up, down, begin, count, before):
    rows, d = shared.shape
    local, _, hid = up.shape
    sub = min(rows, 512)
    here = lambda e, r: (begin + e, r, 0)
    there = lambda e, r: (begin + e, 0, 0)
    wide = jax.ShapeDtypeStruct((local, rows, hid), BF16)
    return pl.pallas_call(
        forward_kernel,
        grid=(count, rows // sub),
        in_specs=[
            pl.BlockSpec((sub, d), lambda e, r: (r, 0)),
            pl.BlockSpec((1, d, hid), there),
            pl.BlockSpec((1, hid, d), there),
        ]
        + [pl.BlockSpec(memory_space=pl.ANY) for _ in before],
        out_specs=[
            pl.BlockSpec((1, sub, hid), here),
            pl.BlockSpec((1, sub, hid), here),
            pl.BlockSpec((1, sub, d), here),
        ],
        out_shape=[wide, wide, jax.ShapeDtypeStruct((local, rows, d), BF16)],
        input_output_aliases={3 + k: k for k in range(len(before))},
        **params(4 * rows * d * hid * count, "forward"),
    )(shared, up, down, *before)


def same_row(n, m, group):
    row = lax.broadcasted_iota(jnp.int32, (n, m), 0) & (group - 1)
    lane = lax.broadcasted_iota(jnp.int32, (1, m), 1) & (group - 1)
    return jnp.where(row == lane, 1.0, 0.0)


def chosen(ids_ref, order, by_task, tasks, local, experts, cols, group):
    wide = tasks * local * group
    lane = shift(lax.broadcasted_iota(jnp.int32, (1, wide), 1), group)
    task = shift(lane, local) if by_task else lane & (tasks - 1)
    expert = lane & (local - 1) if by_task else shift(lane, tasks)
    ids = jnp.zeros_like(lane) + ids_ref[order]
    for t in range(1, tasks):
        ids = jnp.where(task == t, ids_ref[order + t], ids)
    row = lax.broadcasted_iota(jnp.int32, (cols, wide), 0)
    return jnp.where(row == ids * experts + ids_ref[0] + expert, 1.0, 0.0).astype(BF16)


def stack(weights, r, group, count, width):
    return jnp.concatenate(
        [weights[r : r + group, j * width : (j + 1) * width] for j in range(count)], axis=0
    )


def mix_kernel(tasks, experts, block, ids_ref, gates_ref, outs_ref, keep_ref, send_ref):
    i = pl.program_id(0)
    rows, cols = gates_ref.shape
    local = outs_ref.shape[0]
    group = 256 // local
    flat = same_row(block, tasks * local * group, group)
    step = rows // block

    def write(ref):
        for k in range(step):
            at = pl.ds(k * block, block)
            order = 1 + 2 * tasks * (i * step + k) + tasks
            weights = mm(
                gates_ref[at, :].astype(BF16),
                chosen(ids_ref, order, True, tasks, local, experts, cols, group),
            )
            weights = (weights * flat).astype(BF16)
            for r in range(0, block, group):
                part = pl.ds(k * block + r, group)
                out = jnp.concatenate([outs_ref[j, part, :] for j in range(local)], axis=0)
                both = mm(stack(weights, r, group, tasks, local * group), out).astype(BF16)
                for t in range(tasks):
                    ref[t, part, :] = both[t * group : (t + 1) * group]

    pl.when(i < pl.num_programs(0) // 2)(lambda: write(keep_ref))
    pl.when(i >= pl.num_programs(0) // 2)(lambda: write(send_ref))


def mix(ids, gates, outs, n, tasks):
    local, rows, d = outs.shape
    cols = gates.shape[1]
    sub = rows // 4
    return pl.pallas_call(
        functools.partial(mix_kernel, tasks, cols // tasks, rows // n),
        grid_spec=pltpu.PrefetchScalarGridSpec(
            num_scalar_prefetch=1,
            grid=(4,),
            in_specs=[
                pl.BlockSpec((sub, cols), lambda i, f: (i, 0)),
                pl.BlockSpec((local, sub, d), lambda i, f: (0, i, 0)),
            ],
            out_specs=[
                pl.BlockSpec((tasks, sub, d), lambda i, f: (0, jnp.minimum(i, 1), 0)),
                pl.BlockSpec((tasks, sub, d), lambda i, f: (0, jnp.maximum(i - 2, 0), 0)),
            ],
        ),
        out_shape=[jax.ShapeDtypeStruct((tasks, rows // 2, d), BF16)] * 2,
        **params(2**11 * rows * d, "mix"),
    )(ids, gates, outs)


def spread_kernel(tasks, experts, places, n_grads, begin, ids_ref, *refs):
    grads = refs[:n_grads]
    gates_ref, outs_ref = refs[n_grads : n_grads + 2]
    og_ref, inner_ref, rows_ref, sems = refs[-4:]
    i = pl.program_id(0)
    rows, cols = gates_ref.shape
    count = rows_ref.shape[1]
    block = rows // count
    local = og_ref.shape[0]
    group = 256 // local

    def fetch(step, slot, act):
        for k in range(len(places) // count):

            @pl.when(step == k)
            def _():
                for j in range(count):
                    for t, (which, *lead) in enumerate(places[k * count + j]):
                        act(
                            pltpu.make_async_copy(
                                grads[which].at[tuple(lead)],
                                rows_ref.at[slot, j, t],
                                sems.at[slot, j, t],
                            )
                        )

    @pl.when(i == 0)
    def _():
        fetch(0, 0, lambda copy: copy.start())

    fetch(i + 1, (i + 1) & 1, lambda copy: copy.start())
    flat = same_row(block, tasks * local * group, group)
    square = same_row(tasks * group, local * group, group)
    fetch(i, i & 1, lambda copy: copy.wait())
    slot = i & 1
    for k in range(count):
        order = 1 + 2 * tasks * ((begin + i) * count + k)
        at = pl.ds(k * block, block)
        gates = gates_ref[at, :]
        pick = lambda by_task: chosen(
            ids_ref, order, by_task, tasks, local, experts, cols, group
        )
        weights = (mm(gates.astype(BF16), pick(False)) * flat).astype(BF16)
        inners = []
        for r in range(0, block, group):
            part = pl.ds(k * block + r, group)
            grad = jnp.concatenate(
                [rows_ref[slot, k, t, r : r + group, :] for t in range(tasks)], axis=0
            )
            out = jnp.concatenate([outs_ref[j, part, :] for j in range(local)], axis=0)
            both = mm(stack(weights, r, group, local, tasks * group), grad).astype(BF16)
            for j in range(local):
                og_ref[j, part, :] = both[j * group : (j + 1) * group]
            products = mm(grad, out, NT) * square
            inners.append(
                jnp.concatenate(
                    [products[t * group : (t + 1) * group] for t in range(tasks)], axis=1
                )
            )
        inner = jnp.concatenate(inners, axis=0)
        high = inner.astype(BF16)
        rest = (inner - high.astype(F32)).astype(BF16)
        at_column = pick(True)
        inner_ref[at, :] = mm(high, at_column, NT) + mm(rest, at_column, NT)


def spread_grads(ids, grads, places, gates, outs, begin, before, tasks):
    local, rows, d = outs.shape
    cols = gates.shape[1]
    n = len(places)
    count = 1
    block = rows // 2 // n
    sub = count * block
    begin = begin * (n // count)
    every = lambda i, f: (0, begin + i, 0)
    here = lambda i, f: (begin + i, 0)
    return pl.pallas_call(
        functools.partial(spread_kernel, tasks, cols // tasks, places, len(grads), begin),
        grid_spec=pltpu.PrefetchScalarGridSpec(
            num_scalar_prefetch=1,
            grid=(n // count,),
            in_specs=[pl.BlockSpec(memory_space=pl.ANY) for _ in grads]
            + [pl.BlockSpec((sub, cols), here), pl.BlockSpec((local, sub, d), every)]
            + [pl.BlockSpec(memory_space=pl.ANY) for _ in before],
            out_specs=[
                pl.BlockSpec((local, sub, d), every),
                pl.BlockSpec((sub, cols), here),
            ],
            scratch_shapes=[
                pltpu.VMEM((2, count, tasks, block, d), BF16),
                pltpu.SemaphoreType.DMA((2, count, tasks)),
            ],
        ),
        out_shape=[
            jax.ShapeDtypeStruct((local, rows, d), BF16),
            jax.ShapeDtypeStruct((rows, cols), F32),
        ],
        input_output_aliases={3 + len(grads) + k: k for k in range(len(before))},
        **params(2**10 * rows * d, "spread_grads"),
    )(ids, *grads, gates, outs, *before)


def backward_kernel(tasks, experts, n, sub, start, last, ids_ref, *refs):
    og_ref, slope_ref, up_ref, down_ref = refs[:4]
    total_ref = None if start else refs[4]
    if last:
        gates_ref, inner_ref = refs[5 - start : 7 - start]
        pg_ref, keep_ref, send_ref, acc_ref, pair_ref = refs[-5:]
    else:
        pg_ref, acc_ref = refs[-2:]
    e = pl.program_id(0)
    rows, d = acc_ref.shape

    for r in range(0, rows, sub):
        part = pl.ds(r, sub)
        hidden = mm(og_ref[0, part, :], down_ref[0], NT)
        pre_grad = (hidden * slope_ref[0, part, :].astype(F32)).astype(BF16)
        pg_ref[0, part, :] = pre_grad
        found = mm(pre_grad, up_ref[0], NT)

        @pl.when(e == 0)
        def _():
            acc_ref[part, :] = found if start else total_ref[part, :] + found

        @pl.when(e > 0)
        def _():
            acc_ref[part, :] += found

    if not last:
        return
    cols = gates_ref.shape[1]
    block = rows // n
    quarter = block // tasks

    @pl.when(e == 0)
    def _():
        gates, inner = gates_ref[...], inner_ref[...]
        logit = gates * (inner - group_sum(gates * inner, experts))
        high = logit.astype(BF16)
        rest = (logit - high.astype(F32)).astype(BF16)
        row = lax.broadcasted_iota(jnp.int32, (cols, 2 * cols), 0)
        lane = lax.broadcasted_iota(jnp.int32, (cols, 2 * cols), 1)
        one = jnp.where(lane == row, 1.0, 0.0).astype(BF16)
        two = jnp.where(lane == row + cols, 1.0, 0.0).astype(BF16)
        pair_ref[...] = (mm(high, one) + mm(rest, two)).astype(BF16)

    @pl.when(e == pl.num_programs(0) - 1)
    def _():
        for i in range(n):
            ref = keep_ref if i < n // 2 else send_ref
            for t in range(tasks):
                place = ids_ref[1 + 2 * tasks * i + tasks + t]
                begin = pl.multiple_of(i * block + place * quarter, quarter)
                source = pl.ds(begin, quarter)
                dest = pl.ds(i % (n // 2) * quarter, quarter)
                ref[t, dest, :d] = acc_ref[source, :].astype(BF16)
                ref[t, dest, d:] = pair_ref[source, :]


def backward(ids, og, slope, up, down, gates, inner, n, begin, count, before, last, tasks):
    local, rows, d = og.shape
    hid = up.shape[2]
    here = lambda e, f: (begin + e, 0, 0)
    cols = gates.shape[1]
    width = d + 2 * cols
    packed = (tasks, rows // 2 // tasks, width)
    start = before is None
    whole = lambda shape, **how: pl.BlockSpec(shape, lambda e, f: (0,) * len(shape), **how)
    specs, shapes, scratch = [whole((rows, d))], [jax.ShapeDtypeStruct((rows, d), F32)], []
    if last:
        specs, shapes = [whole(packed)] * 2, [jax.ShapeDtypeStruct(packed, BF16)] * 2
        scratch = [pltpu.VMEM((rows, d), F32), pltpu.VMEM((rows, 2 * cols), BF16)]
    args, in_specs = [], []
    if not start:
        args, in_specs = [before[1]], [whole((rows, d), pipeline_mode=pl.Buffered(1))]
    if last:
        args, in_specs = args + [gates, inner], in_specs + [whole((rows, cols))] * 2
    if not start:
        args, in_specs = args + [before[0]], in_specs + [pl.BlockSpec(memory_space=pl.ANY)]
    return pl.pallas_call(
        functools.partial(
            backward_kernel, tasks, cols // tasks, n, min(rows, 1024), start, last
        ),
        grid_spec=pltpu.PrefetchScalarGridSpec(
            num_scalar_prefetch=1,
            grid=(count,),
            in_specs=[
                pl.BlockSpec((1, rows, d), here),
                pl.BlockSpec((1, rows, hid), here),
                pl.BlockSpec((1, d, hid), here),
                pl.BlockSpec((1, hid, d), here),
            ]
            + in_specs,
            out_specs=[pl.BlockSpec((1, rows, hid), here)] + specs,
            scratch_shapes=scratch,
        ),
        out_shape=[jax.ShapeDtypeStruct((local, rows, hid), BF16)] + shapes,
        input_output_aliases={} if start else {4 + len(args): 0},
        **params(4 * rows * d * hid * count, "backward"),
    )(ids, og, slope, up, down, *args)


def weights_kernel(n, *refs):
    shared, acts, ogs, pgs = (refs[k * n : (k + 1) * n] for k in range(4))
    up_ref, down_ref = refs[-2:]
    total = sum(mm(s[...], p[0], TN) for s, p in zip(shared, pgs))
    up_ref[0] = total.astype(BF16)
    total = sum(mm(a[0], o[0], TN) for a, o in zip(acts, ogs))
    down_ref[0] = total.astype(BF16)


def weight_grads(shared, acts, ogs, pgs, begin, count, before):
    local, rows, hid = acts[0].shape
    d = shared[0].shape[1]
    n = len(shared)
    there = lambda e, h: (begin + e, 0, 0)
    half = [pl.BlockSpec((1, x.shape[1], hid // 2), lambda e, h: (begin + e, 0, h)) for x in acts]
    return pl.pallas_call(
        functools.partial(weights_kernel, n),
        grid=(count, 2),
        in_specs=[pl.BlockSpec(s.shape, lambda e, h: (0, 0)) for s in shared]
        + half
        + [pl.BlockSpec((1,) + x.shape[1:], there) for x in ogs]
        + half
        + [pl.BlockSpec(memory_space=pl.ANY) for _ in before],
        out_specs=[
            pl.BlockSpec((1, d, hid // 2), lambda e, h: (begin + e, 0, h)),
            pl.BlockSpec((1, hid // 2, d), lambda e, h: (begin + e, h, 0)),
        ],
        out_shape=[
            jax.ShapeDtypeStruct((local, d, hid), BF16),
            jax.ShapeDtypeStruct((local, hid, d), BF16),
        ],
        input_output_aliases={4 * n + k: k for k in range(len(before))},
        **params(4 * n * rows * d * hid * count, "weight_grads"),
    )(*shared, *acts, *ogs, *pgs, *before)


def rows_kernel(tasks, cols, bases, sizes, ids_ref, *refs):
    n = len(bases)
    parts, pairs = refs[:n], refs[n : 2 * n]
    feat_ref, tile_ref, shared_ref = refs[2 * n : 2 * n + 3]
    cross_ref, bias_ref, gating_ref, offset_ref, every_ref, pair_ref = refs[2 * n + 3 :]
    for k, (base, (half, slot)) in enumerate(zip(bases, sizes)):
        shares, blocks, quarter, _ = parts[k].shape
        block = quarter * tasks
        for s in range(shares):
            place = ids_ref[1 + (2 - half) * tasks + slot + s] * quarter
            for j in range(blocks):
                rows = pl.ds(pl.multiple_of(base + j * block + place, quarter), quarter)
                every_ref[rows, :] = parts[k][s, j]
                pair_ref[rows, :] = pairs[k][s, j]
    scaled = (every_ref[...].astype(F32) * tile_ref[...].astype(F32)).astype(BF16)
    cross_ref[...] = mm(feat_ref[...], scaled, TN)
    bias_ref[...] = jnp.sum(scaled.astype(F32), axis=0, keepdims=True)
    pair = pair_ref[...]
    gating_ref[...] = mm(pair[:, :cols], shared_ref[...], TN)
    offset = jnp.sum(pair.astype(F32), axis=0, keepdims=True)
    offset_ref[...] = offset[:, :cols] + offset[:, cols:]


def rows_grads(ids, found, feat, shared, cols, tasks):
    rows, d = feat.shape
    tile = 512
    parts, bases, sizes = [], [], []
    for half, (base, some) in enumerate(found):
        slot = 0
        for part in some:
            parts.append(part)
            bases.append(base)
            sizes.append((half % 2, slot))
            slot += part.shape[0]
    wide = parts[0].shape[-1] - d
    column = lambda j: (0, j)
    return pl.pallas_call(
        functools.partial(rows_kernel, tasks, cols, bases, sizes),
        grid=(d // tile,),
        in_specs=[pl.BlockSpec(memory_space=pltpu.SMEM)]
        + [pl.BlockSpec(p.shape[:3] + (tile,), lambda j: (0, 0, 0, j)) for p in parts]
        + [pl.BlockSpec(p.shape[:3] + (wide,), lambda j: (0, 0, 0, d // wide)) for p in parts]
        + [
            pl.BlockSpec((rows, d), lambda j: (0, 0), pipeline_mode=pl.Buffered(1)),
            pl.BlockSpec((rows, tile), column),
            pl.BlockSpec((rows, tile), column),
        ],
        out_specs=[
            pl.BlockSpec((d, tile), column),
            pl.BlockSpec((1, tile), column),
            pl.BlockSpec((cols, tile), column),
            pl.BlockSpec((1, cols), lambda j: (0, 0)),
        ],
        out_shape=[
            jax.ShapeDtypeStruct((d, d), F32),
            jax.ShapeDtypeStruct((1, d), F32),
            jax.ShapeDtypeStruct((cols, d), F32),
            jax.ShapeDtypeStruct((1, cols), F32),
        ],
        scratch_shapes=[pltpu.VMEM((rows, tile), BF16), pltpu.VMEM((rows, wide), BF16)],
        **params(2 * rows * d * d, "rows_grads"),
    )(ids, *parts, *parts, feat, feat, shared)


def added(parts):
    return sum(p.astype(F32) for p in parts)


class Ring:
    def __init__(self, dp, expert):
        size = dp * expert

        def pairs(move):
            found = []
            for i in range(size):
                z, c, q = i // expert // 2, i // expert % 2, i % expert
                z, c, q = move(z, c, q)
                found.append((i, (z * 2 + c) * expert + q))
            return found

        self.core_pairs = pairs(lambda z, c, q: (z, 1 - c, q))
        self.z1_pairs = pairs(lambda z, c, q: (z ^ 1, c, q))
        self.z3_pairs = pairs(lambda z, c, q: (z ^ 3, c, q))
        self.e1_pairs = pairs(lambda z, c, q: (z, c, q ^ (1, 2)[c]))
        self.e2_pairs = pairs(lambda z, c, q: (z, c, q ^ (2, 1)[c]))

        places = [tuple((0, t) for t in range(4))]
        for k, j in ((1, 0), (4, 0), (4, 1)):
            places.append(((k, 0, j), (k + 1, 0, j), (k + 2, 0, j), (k + 2, 1, j)))
        self.places, self.blocks = tuple(places), 8

    def move(self, x, pairs):
        return lax.ppermute(x, ("dp", "expert"), pairs)

    def core(self, x):
        return self.move(x, self.core_pairs)

    def orders(self):
        q, c = lax.axis_index("expert"), lax.axis_index("dp") % 2
        b1, b2 = 1 + c, 2 - c
        return [q, q ^ b2, q ^ b1, q ^ 3], [q, q ^ b1, q ^ b2, q ^ 3]

    def ids(self, first, tasks):
        mine, other = self.orders()
        plain = list(range(tasks))
        ids = [first]
        for order in (mine, other):
            for k in range(4):
                ids += plain if k == 0 else (other if order is mine else mine)
                ids += order
        return [jnp.stack([jnp.asarray(i, jnp.int32) for i in ids])]

    def spread(self, x):
        one = self.move(x, self.e1_pairs)
        rest = self.move(jnp.stack([x, one]), self.e2_pairs)
        return x[None], one[None], rest

    def in_order(self, parts, order):
        parts = jnp.concatenate(parts, axis=0)
        place = lambda share: sum(jnp.where(order[i] == share, i, 0) for i in range(4))
        return [lax.dynamic_index_in_dim(parts, place(i), 0, False) for i in range(4)]

    def rows(self, x):
        three, one = self.move(x, self.z3_pairs), self.move(x, self.z1_pairs)
        three, one = lax.optimization_barrier((three, one))
        mine = [x, three, one]
        last = self.move(three, self.z1_pairs)
        both = lambda parts: parts + [self.core(p) for p in parts]
        return [[both(mine), lambda *after: both([tie(last, *after)])]], one, last

    def grads(self, task_grad):
        own = jnp.transpose(task_grad, (1, 0, 2))
        share = lax.dynamic_index_in_dim(task_grad, lax.axis_index("expert"), 1, False)
        core, move = self.core, self.move
        share, own = yield (share, own)
        three, own2 = yield (move(share, self.z3_pairs), core(own))
        a0 = three[None]
        both, a0 = yield (jnp.stack([share, three]), a0)
        b0, a1 = yield (move(both, self.z1_pairs), move(a0, self.e1_pairs))
        b0, out = yield (b0, jnp.stack([a0, a1]))
        b1, a2 = yield (move(b0, self.e1_pairs), move(out, self.e2_pairs))
        out, *a = yield (jnp.stack([b0, b1]), a0, a1, a2)
        b2, *other_a = yield (move(out, self.e2_pairs), *map(core, a))
        lift = lambda x, y, z: [x[None], y[None], z]
        self.near = [[own, *lift(*a), *lift(b0, b1, b2)]]
        b = yield (b0, b1, b2)
        other_b = yield tuple(map(core, b))
        far = [own2, *lift(*other_a), *lift(*other_b)]
        return self.near, [far], self.places

    def reduce(self, parts, scatter):
        ((keep, send),) = parts
        (out,) = yield (send,)
        (got,) = yield (self.core(out),)
        parts = [keep, got]
        (out,) = yield (added([p[2:] for p in parts]).astype(BF16),)
        (got,) = yield (self.move(out, self.e1_pairs),)
        parts = [p[:2] for p in parts] + [got]
        (out,) = yield (added([p[1] for p in parts]).astype(BF16),)
        (got,) = yield (self.move(out, self.e2_pairs),)
        parts = [p[0] for p in parts] + [got]
        half = got.shape[0] // 2
        if scatter:
            (out,) = yield (added([p[half:] for p in parts]).astype(BF16),)
            (got,) = yield (self.move(out, self.z1_pairs),)
            parts = [p[:half] for p in parts] + [got]
            half = half // 2
            (out,) = yield (added([p[half:] for p in parts]).astype(BF16),)
            (got,) = yield (self.move(out, self.z3_pairs),)
            return added([p[:half] for p in parts] + [got])
        shape = (4, -1, got.shape[-1])
        (out,) = yield (added(parts).astype(BF16).reshape(shape),)
        (got,) = yield (self.move(out, self.z1_pairs),)
        out = added([out, jnp.concatenate([got[2:], got[:2]], axis=0)])
        (out,) = yield (out.astype(BF16),)
        (got,) = yield (self.move(out, self.z3_pairs),)
        return added([out, jnp.stack([got[1], got[0], got[3], got[2]])])

    def share_tasks(self, x):
        return self.in_order(self.spread(x), self.orders()[1])

    def share_rows(self, x):
        mine = self.spread(x)
        own = jnp.concatenate(self.in_order([m[:, 0] for m in mine], self.orders()[1]), axis=0)
        other = [self.core(p) for p in mine]
        block = x.shape[1] * 4
        return [(0, mine), (4 * block, other)], own


class Steps:
    def __init__(self, steps):
        self.steps, self.moved, self.value = steps, None, None
        self.operand = self._next(None)

    def _next(self, sent):
        try:
            return self.steps.send(sent)
        except StopIteration as stop:
            self.value = stop.value

    def start(self, *after):
        if self.operand is not None:
            self.moved, self.operand = self._next(tie(self.operand, *after)), None

    def finish(self, *after):
        if self.moved is not None:
            moved, self.moved = self.moved, None
            self.operand = self._next(tie(moved, *after))

    def result(self):
        while self.moved is not None or self.operand is not None:
            self.start()
            self.finish()
        return self.value


def finish(steps, *after):
    moved = tie([s.moved or () for s in steps], *after)
    earlier = None
    for one, arrays in zip(steps, moved):
        if one.moved is not None:
            one.moved = arrays
            one.finish(earlier)
            earlier = one.operand


def tie(x, *others):
    others = [o for o in others if o is not None]
    return lax.optimization_barrier((x, *others))[0] if others else x


class Plain:
    def __init__(self, dp, expert):
        self.dp = dp
        self.count = dp // 8 if dp % 8 == 0 else 1
        self.blocks = dp // self.count

    def ids(self, first, tasks):
        plain = list(range(tasks)) * 2 * self.blocks
        return [jnp.stack([jnp.asarray(i, jnp.int32) for i in (first, *plain)])] * self.count

    def rows(self, x):
        every = lax.all_gather(x, "dp", axis=0, tiled=True)
        blocks = jnp.split(every, self.dp)
        n = self.blocks
        return [[blocks[i : i + n]] for i in range(0, self.dp, n)], None, None

    def grads(self, task_grad):
        every = lax.all_gather(jnp.transpose(task_grad, (1, 0, 2)), "dp", axis=0)
        tasks, half = task_grad.shape[1], self.blocks // 2
        self.places = tuple(tuple((0, i, t) for t in range(tasks)) for i in range(half))
        parts = jnp.split(every, 2 * self.count)
        self.near = [[p] for p in parts[::2]]
        return self.near, [[p] for p in parts[1::2]], self.places
        yield

    def reduce(self, parts, scatter):
        blocks = []
        for part in (p for pair in parts for p in pair):
            part = part.reshape(part.shape[0], self.blocks // 2, -1, part.shape[-1])
            blocks.append(jnp.swapaxes(part.astype(F32), 0, 1))
        blocks = jnp.concatenate(blocks, axis=0)
        own = lax.psum_scatter(blocks, "dp", scatter_dimension=0, tiled=True)[0]
        return lax.psum(own, "expert")
        yield

    def share_tasks(self, x):
        return list(x)

    def share_rows(self, x):
        every = jnp.swapaxes(lax.all_gather(x, "dp", axis=0), 0, 1)
        shares, _, quarter, d = every.shape
        found = []
        for k, part in enumerate(jnp.split(every, 2 * self.count, axis=1)):
            found.append((k * self.blocks // 2 * quarter * shares, [part]))
        return found, x.reshape(-1, d)


def local_step(
    net, features, cross_weight, cross_bias, gate_weight, gate_offset, up_weight, down_weight,
    task_grad,
):
    block, d = features.shape
    tasks = task_grad.shape[1]
    cols = gate_weight.shape[1]
    local = up_weight.shape[0]
    first = lax.axis_index("expert") * local
    ids = net.ids(first, tasks)

    feats, early, late = net.rows(features)
    grads = Steps(net.grads(task_grad))
    grads.start(early)

    lowered = []
    for pieces in feats:
        found, begin = (), 0
        for piece in pieces:
            piece = piece(*found, grads.moved) if callable(piece) else piece
            found = cross(
                piece, cross_weight[0], cross_bias, gate_weight.T, gate_offset[None],
                net.blocks // 2, begin, found, tasks,
            )
            begin += len(piece) // 2
        lowered.append(found)
    feats, shared, gates = zip(*lowered)
    grads.finish(*shared)
    ready = grads.operand
    grads.start()
    done = [() for _ in shared]
    quarter = local // 4
    sizes = (local - 2 * quarter, quarter, quarter) if quarter else (local,)
    begins = list(itertools.accumulate((0, *sizes)))
    for b, size in zip(begins, sizes):
        if b:
            grads.finish(*[found[0] for found in done])
            ready = grads.operand
            grads.start()
        done = [
            forward(tie(low, ready), up_weight, down_weight, b, size, found)
            for low, found in zip(shared, done)
        ]
    acts, slopes, outs = zip(*done)
    grads.finish(*[found[0] for found in done])
    ready = grads.operand
    grads.start()
    n = net.blocks
    mixed = [mix(i, tie(gt, ready), o, n, tasks) for i, gt, o in zip(ids, gates, outs)]
    grads.finish(*[keep for keep, _ in mixed])
    near, places = net.near, net.places
    ready = grads.operand
    grads.start()
    mixed = Steps(net.reduce(mixed, True))
    mixed.start()
    spread = [
        spread_grads(i, g, places, tie(gt, ready), o, 0, (), tasks)
        for i, g, gt, o in zip(ids, near, gates, outs)
    ]
    finish([grads, mixed], *[og for og, _ in spread])
    far = grads.result()[1]
    spread = [
        spread_grads(i, g, places, gt, o, 1, tie(x, mixed.operand), tasks)
        for i, g, gt, o, x in zip(ids, far, gates, outs, spread)
    ]
    back = [None for _ in spread]
    parts = BACKWARD_PARTS if local % BACKWARD_PARTS == 0 else 1
    for k in range(parts):
        ready = mixed.operand
        mixed.start()
        back = [
            backward(
                i, tie(og, ready), slope, up_weight, down_weight, gt, inner, n,
                k * local // parts, local // parts, before, k == parts - 1, tasks,
            )
            for i, (og, inner), slope, gt, before in zip(ids, spread, slopes, gates, back)
        ]
        if k < parts - 1:
            mixed.finish(*[x[0] for x in back])
    ogs = [og for og, _ in spread]
    pgs = [b[0] for b in back]
    total = Steps(net.reduce(tie([b[1:] for b in back], mixed.moved), False))
    total.start()
    total.finish()
    mixed.finish(*pgs)
    weights = ()
    for b, size in zip(begins, sizes):
        ready = (mixed.operand, total.operand)
        total.start()
        mixed.start()
        tied = [tie(a, *ready) for a in acts]
        weights = weight_grads(shared, tied, ogs, pgs, b, size, weights)
        if b + size < local:
            finish([total, mixed], weights[0])
        else:
            total.finish(weights[0])
            mixed.finish(weights[0], total.operand)
    up_grad, down_grad = weights
    total = total.result()
    task_mixed = mixed.result().astype(BF16)
    task_mixed = jnp.stack(net.share_tasks(task_mixed), axis=1)

    logit = total[..., d : d + cols] + total[..., d + cols :]
    high = logit.astype(BF16)
    low = (logit - high.astype(F32)).astype(BF16)
    upstream = total[..., :d] + lax.dot_general(
        high, gate_weight, (((high.ndim - 1,), (1,)), ((), ())), preferred_element_type=F32
    )
    every, own = net.share_rows(jnp.concatenate([upstream.astype(BF16), high, low], axis=-1))
    feats, shared = (x[0] if len(x) == 1 else jnp.concatenate(x, axis=0) for x in (feats, shared))
    cross_grad, bias_grad, gating_grad, offset_grad = rows_grads(
        ids[0], every, feats, shared, cols, tasks
    )

    update = mm(features, cross_weight[0]) + cross_bias
    upstream = own[:, :d].astype(F32)
    scaled = (upstream * features.astype(F32)).astype(BF16)
    feature_grad = (upstream + mm(scaled, cross_weight[0], NT) + upstream * update).astype(BF16)
    return (
        task_mixed,
        feature_grad,
        up_grad,
        down_grad,
        cross_grad[None],
        bias_grad,
        gating_grad.T,
        offset_grad[0],
    )


def solution(mesh):
    dp, expert = mesh.shape["dp"], mesh.shape["expert"]
    net = (Ring if (dp, expert) == (8, 4) else Plain)(dp, expert)
    return jax.shard_map(
        functools.partial(local_step, net),
        mesh=mesh,
        in_specs=(
            P("dp", None),
            P(),
            P(),
            P(),
            P(),
            P("expert", None, "dp"),
            P("expert", "dp", None),
            P("dp", None, None),
        ),
        out_specs=(
            P("dp", None, None),
            P("dp", None),
            P("expert", None, "dp"),
            P("expert", "dp", None),
            P(),
            P(),
            P(),
            P(),
        ),
        check_vma=False,
    )
```
